512 devices in a mesh: row: 16 (over z, core), col: 8 (over y), layer: 4 (over x).
Axes of the slice: x: 4, y: 8, z: 8, core: 2. Of those that a mesh axis runs over, the one named last changes fastest.
Arguments:
- slab_panel: bfloat16 [8192, 4, 4096], P('row', 'layer', 'col'), may hold values from -0.59765625 to 0.59765625
- slab_pattern: int32 [32, 4, 16], P('row', 'layer', 'col'), may hold values 0 or 1
- inner_panel: bfloat16 [4, 4096, 4096], P('layer', 'row', 'col'), may hold values from -0.59765625 to 0.59765625
- inner_pattern: int32 [4, 16, 16], P('layer', 'row', 'col'), may hold values 0 or 1
- slab_rows: int32 [32], P('row'), may hold values from 0 to 63
- column_ids: int32 [16], P('col'), may hold values from 0 to 63
Outputs:
- square_slab: bfloat16 [8192, 4096], P('row', ('col', 'layer'))
The draws below stay inside these ranges and needn't reach their ends.
All inputs are finite; a program needn't handle non-finite values. No bound on the sum of `slab_pattern` or of `inner_pattern` on one device may be relied on, other than what follows from the above.
Results may differ from the reference program's by a relative error of at most 0.001.
Values may be sent and summed in bfloat16 or wider, within the bound.
A program may use at most 64 MiB of HBM per device.

```python
import jax
import jax.numpy as jnp

B = 256
NI = 32
NJ = 16
NL = 4
NKL = 16
IDS = 64


def set_ends(entries, key, least, top_value):
    spot = [jax.random.randint(jax.random.fold_in(key, axis), (), 0, length) for axis, length in enumerate(entries.shape)]
    main_axis = entries.shape.index(max(entries.shape))
    next_to = spot[:main_axis] + [(spot[main_axis] + 1) % entries.shape[main_axis]] + spot[main_axis + 1:]
    return entries.at[tuple(spot)].set(least).at[tuple(next_to)].set(top_value)


def steps_of(rng, dims, pieces, least, top_value):
    def one(axis_at, blocks):
        draws = jax.random.uniform(jax.random.fold_in(jax.random.fold_in(rng, 6), axis_at), (blocks,), jnp.float32, least / len(pieces), top_value / len(pieces))
        return jnp.repeat(jnp.exp(draws), dims[axis_at] // blocks).reshape((-1,) + (1,) * (len(dims) - axis_at - 1))

    loudness = one(*pieces[0])
    for cut in pieces[1:]:
        loudness = loudness * one(*cut)
    return loudness


def scatter_about(rng, extent, scale, limit, pieces=(), held_as=jnp.bfloat16):
    result = scale * jax.random.normal(rng, extent, jnp.float32)
    if pieces:
        result = result * steps_of(rng, extent, pieces, -0.22, 0.18)
    return jnp.clip(result, -limit, limit).astype(held_as)


def setup_inputs(seed: int = 0) -> dict:
    seeds = jax.random.split(jax.random.key(seed), 7)
    return {
        "slab_panel": scatter_about(seeds[0], (NI * B, NL, NKL * B), 0.1, 0.59765625, ((0, 16), (1, 4), (2, 8))),
        "slab_pattern": set_ends((jax.random.randint(seeds[1], (NI, NL, NKL), 0, 2) < 1).astype(jnp.int32), jax.random.fold_in(seeds[1], 1), 0, 1),
        "inner_panel": scatter_about(seeds[2], (NL, NKL * B, NJ * B), 0.1, 0.59765625, ((0, 4), (1, 16), (2, 8))),
        "inner_pattern": set_ends((jax.random.randint(seeds[3], (NL, NKL, NJ), 0, 2) < 1).astype(jnp.int32), jax.random.fold_in(seeds[3], 1), 0, 1),
        "slab_rows": set_ends(jax.random.randint(seeds[4], (NI,), 0, IDS), jax.random.fold_in(seeds[4], 1), 0, IDS - 1).astype(jnp.int32),
        "column_ids": set_ends(jax.random.randint(seeds[5], (NJ,), 0, IDS), jax.random.fold_in(seeds[5], 1), 0, IDS - 1).astype(jnp.int32),
    }


def apply_pattern(panel, pattern):
    blocks_down, blocks_across = pattern.shape
    block_width = panel.shape[0] // blocks_down
    spread = panel.reshape(blocks_down, block_width, blocks_across, block_width) * pattern.astype(panel.dtype)[:, None, :, None]
    return spread.reshape(panel.shape)


def reference(slab_panel, slab_pattern, inner_panel, inner_pattern, slab_rows, column_ids):
    block_width = slab_panel.shape[0] // slab_pattern.shape[0]
    tile_sum = jnp.zeros((slab_panel.shape[0], inner_panel.shape[2]), jnp.float32)
    for part_index in range(NL):
        masked_a = apply_pattern(slab_panel[:, part_index, :], slab_pattern[:, part_index, :])
        masked_b = apply_pattern(inner_panel[part_index], inner_pattern[part_index])
        tile_sum = tile_sum + jnp.dot(masked_a, masked_b, preferred_element_type=jnp.float32)
    keep_cells = (column_ids[None, :] >= slab_rows[:, None]).astype(jnp.float32)
    keep_full = jnp.repeat(jnp.repeat(keep_cells, block_width, axis=0), block_width, axis=1)
    return (tile_sum * keep_full).astype(jnp.bfloat16)
```

```python
import functools

import jax
import jax.numpy as jnp
from jax import lax
from jax.experimental import pallas as pl
from jax.experimental.pallas import tpu as pltpu
from jax.sharding import PartitionSpec as P

MESH = pl.DeviceIdType.MESH
BW = 256
NY, NZ, NX = 8, 8, 4
Q = 4
PIECE = 512 // Q
HALF = PIECE // 2
PHASES = 2


def kernel(slab, slab_pat, inner, inner_pat, rows_ids, col_ids, out,
           a_raw, b_raw, a_all, b_all, acc, rs,
           ld_sem, as_sem, ar_sem, bs_sem, br_sem, ss_sem, sr_sem, cs_sem, cr_sem):
    r, y, x = lax.axis_index("row"), lax.axis_index("col"), lax.axis_index("layer")
    z, c = r // 2, r % 2

    def dev(row=r, col=y, layer=x):
        return (row, col, layer)

    y_to = [dev(col=(y + 1) % NY), dev(col=(y + NY - 1) % NY)]
    z_to = [dev(row=((z + 1) % NZ) * 2 + c), dev(row=((z + NZ - 1) % NZ) * 2 + c)]
    sib = dev(row=z * 2 + 1 - c)
    x_to = [dev(layer=(x + d) % NX) for d in range(1, NX)]

    barrier = pltpu.get_barrier_semaphore()
    for peer in y_to + z_to + [sib] + x_to:
        pl.semaphore_signal(barrier, inc=1, device_id=peer, device_id_type=MESH)

    loads = []
    for q in range(Q):
        rows = pl.ds(q * PIECE, PIECE)
        loads.append(pltpu.make_async_copy(slab.at[rows], a_raw.at[rows], ld_sem.at[q]))
    loads.append(pltpu.make_async_copy(inner, b_raw, ld_sem.at[Q]))
    for cp in (loads[0], loads[4], loads[1], loads[2], loads[3]):
        cp.start()

    def mask_a(q):
        loads[q].wait()
        for j in range(2):
            keep = slab_pat[q * PIECE // BW, 0, j].astype(jnp.float32).astype(jnp.bfloat16)
            blk = a_raw[pl.ds(q * PIECE, PIECE), pl.ds(j * BW, BW)]
            a_all[y, pl.ds(q * PIECE, PIECE), pl.ds(j * BW, BW)] = blk * keep

    def mask_b():
        loads[Q].wait()
        for j in range(2):
            keep = inner_pat[0, 0, j].astype(jnp.float32).astype(jnp.bfloat16)
            b_all[z, pl.ds(c * BW, BW), pl.ds(j * BW, BW)] = b_raw[:, pl.ds(j * BW, BW)] * keep

    def y_src(way, d):
        return (y + NY - d) % NY if way == 0 else (y + d) % NY

    def a_copy(way, q, d):
        src = y_src(way, d)
        lo, n = (q * PIECE, PIECE) if d < 3 else (q * PIECE + way * HALF, HALF)
        ref = a_all.at[src, pl.ds(lo, n)]
        return pltpu.make_async_remote_copy(
            src_ref=ref, dst_ref=ref, send_sem=as_sem.at[way, q, d], recv_sem=ar_sem.at[way, q, d],
            device_id=y_to[way], device_id_type=MESH)

    def a_arrive(way, q, d):
        src = y_src(way, d)
        lo, n = (q * PIECE, PIECE) if d < 4 else (q * PIECE + way * HALF, HALF)
        ref = a_all.at[src, pl.ds(lo, n)]
        pltpu.make_async_remote_copy(
            src_ref=ref, dst_ref=ref, send_sem=as_sem.at[way, q, d - 1], recv_sem=ar_sem.at[way, q, d - 1],
            device_id=y_to[way], device_id_type=MESH).wait_recv()

    def z_src(way, d):
        return (z + NZ - d) % NZ if way == 0 else (z + d) % NZ

    def b_ref(way, d, core, part):
        lo, n = (0, BW) if not part else (way * (BW // 2), BW // 2)
        return b_all.at[z_src(way, d), pl.ds(core * BW + lo, n)]

    def b_copy(way, d):
        ref = b_ref(way, d, c, d == 3)
        return pltpu.make_async_remote_copy(
            src_ref=ref, dst_ref=ref, send_sem=bs_sem.at[way, d], recv_sem=br_sem.at[way, d],
            device_id=z_to[way], device_id_type=MESH)

    def b_arrive(way, d):
        ref = b_ref(way, d, c, d == 4)
        pltpu.make_async_remote_copy(
            src_ref=ref, dst_ref=ref, send_sem=bs_sem.at[way, d - 1], recv_sem=br_sem.at[way, d - 1],
            device_id=z_to[way], device_id_type=MESH).wait_recv()

    def s_copy(way, d, core):
        ref = b_ref(way, d, core, d == 4)
        return pltpu.make_async_remote_copy(
            src_ref=ref, dst_ref=ref, send_sem=ss_sem.at[way, d], recv_sem=sr_sem.at[way, d],
            device_id=sib, device_id_type=MESH)

    def c_copy(ph, d):
        return pltpu.make_async_remote_copy(
            src_ref=acc.at[ph, (x + d) % NX], dst_ref=rs.at[ph, d - 1],
            send_sem=cs_sem.at[ph, d - 1], recv_sem=cr_sem.at[ph, d - 1],
            device_id=x_to[d - 1], device_id_type=MESH)

    def mm(ph, src, first=False):
        res = jnp.dot(a_all[src, pl.ds(ph * BW, BW), :], b_all[src], preferred_element_type=jnp.float32)
        for k in range(NX):
            part = res[:, k * 128:(k + 1) * 128]
            if first:
                acc[ph, k] = part
            else:
                acc[ph, k] += part

    def finish(ph):
        for d in range(1, NX):
            c_copy(ph, d).wait_recv()
        total = acc[ph, x] + rs[ph, 0] + rs[ph, 1] + rs[ph, 2]
        keep = col_ids[x // 2] >= rows_ids[ph]
        out[pl.ds(ph * BW, BW), :] = jnp.where(keep, total, 0.0).astype(jnp.bfloat16)

    def a_events(pair, d):
        for q in pair:
            for way in range(2):
                a_arrive(way, q, d)
                if d < 4:
                    a_copy(way, q, d).start()

    def b_events(d):
        for way in range(2):
            b_arrive(way, d)
            if d < 4:
                b_copy(way, d).start()
            s_copy(way, d, c).start()

    mask_a(0)
    pl.semaphore_wait(barrier, 2 + 2 + 1 + NX - 1)
    for way in range(2):
        a_copy(way, 0, 0).start()
    mask_b()
    for way in range(2):
        b_copy(way, 0).start()
    s_copy(0, 0, c).start()
    mask_a(1)
    for way in range(2):
        a_copy(way, 1, 0).start()
    mask_a(2)
    mask_a(3)

    a_events((0, 1), 1)
    b_events(1)
    a_events((0, 1), 2)
    for q in (2, 3):
        for way in range(2):
            a_copy(way, q, 0).start()
    b_events(2)
    a_events((0, 1), 3)
    b_events(3)
    a_events((0, 1), 4)
    a_events((2, 3), 1)
    b_events(4)
    s_copy(0, 0, 1 - c).wait_recv()
    for d in range(1, 5):
        for way in range(2):
            s_copy(way, d, 1 - c).wait_recv()
    mm(0, y, True)
    for d in range(1, 4):
        for way in range(2):
            mm(0, y_src(way, d))
    mm(0, y_src(0, 4))
    for d in range(1, NX):
        c_copy(0, d).start()
    a_events((2, 3), 2)
    mm(1, y, True)
    for d in range(1, 3):
        for way in range(2):
            mm(1, y_src(way, d))
    a_events((2, 3), 3)
    for way in range(2):
        mm(1, y_src(way, 3))
    finish(0)
    a_events((2, 3), 4)
    mm(1, y_src(0, 4))
    for d in range(1, NX):
        c_copy(1, d).start()
    for way in range(2):
        for q in range(Q):
            for d in range(4):
                a_copy(way, q, d).wait_send()
        for d in range(4):
            b_copy(way, d).wait_send()
        for d in range(1, 5):
            s_copy(way, d, c).wait_send()
    s_copy(0, 0, c).wait_send()
    for ph in range(PHASES):
        for d in range(1, NX):
            c_copy(ph, d).wait_send()
    finish(1)


def on_device(slab_panel, slab_pattern, inner_panel, inner_pattern, slab_rows, column_ids):
    any_spec = pl.BlockSpec(memory_space=pl.ANY)
    smem = pl.BlockSpec(memory_space=pltpu.SMEM)
    dma = pltpu.SemaphoreType.DMA
    return pl.pallas_call(
        kernel,
        out_shape=jax.ShapeDtypeStruct((512, 128), jnp.bfloat16),
        in_specs=[any_spec, smem, any_spec, smem, smem, smem],
        out_specs=pl.BlockSpec(memory_space=pltpu.VMEM),
        scratch_shapes=[
            pltpu.VMEM((512, 512), jnp.bfloat16),
            pltpu.VMEM((256, 512), jnp.bfloat16),
            pltpu.VMEM((NY, 512, 512), jnp.bfloat16),
            pltpu.VMEM((NZ, 512, 512), jnp.bfloat16),
            pltpu.VMEM((PHASES, NX, 256, 128), jnp.float32),
            pltpu.VMEM((PHASES, NX - 1, 256, 128), jnp.float32),
            dma((Q + 1,)),
            dma((2, Q, 4)), dma((2, Q, 4)),
            dma((2, 4)), dma((2, 4)),
            dma((2, 5)), dma((2, 5)),
            dma((PHASES, NX - 1)), dma((PHASES, NX - 1)),
        ],
        compiler_params=pltpu.CompilerParams(
            collective_id=0, has_side_effects=True, vmem_limit_bytes=40 * 1024 * 1024),
        cost_estimate=pl.CostEstimate(flops=2 * 512 * 512 * 4096, bytes_accessed=2 << 20, transcendentals=0),
    )(slab_panel.reshape(512, 512), slab_pattern, inner_panel.reshape(256, 512), inner_pattern, slab_rows, column_ids)


def solution(mesh):
    return jax.shard_map(
        on_device,
        mesh=mesh,
        in_specs=(
            P("row", "layer", "col"),
            P("row", "layer", "col"),
            P("layer", "row", "col"),
            P("layer", "row", "col"),
            P("row"),
            P("col"),
        ),
        out_specs=P("row", ("col", "layer")),
        check_vma=False,
    )
```

```python
import jax
import jax.numpy as jnp
from jax import lax
from jax.experimental import pallas as pl
from jax.experimental.pallas import tpu as pltpu
from jax.sharding import PartitionSpec as P

MESH = pl.DeviceIdType.MESH
BW = 256
NY, NZ, NX = 8, 8, 4
SIDE = 512
PIECES = (128, 128, 128, 128)
STARTS = tuple(sum(PIECES[:q]) for q in range(len(PIECES)))
Q = len(PIECES)
PB = 2
BP = BW // PB


def kernel(slab, slab_pat, inner, inner_pat, row_ids, col_ids, out,
           a_raw, b_raw, a_all, b_all, acc, rs,
           ld_sem, as_sem, ar_sem, bs_sem, br_sem, ss_sem, sr_sem, cs_sem, cr_sem):
    r, y, x = lax.axis_index("row"), lax.axis_index("col"), lax.axis_index("layer")
    z, c = r // 2, r % 2
    y_to = [(r, (y + 1) % NY, x), (r, (y + NY - 1) % NY, x)]
    z_to = [(((z + 1) % NZ) * 2 + c, y, x), (((z + NZ - 1) % NZ) * 2 + c, y, x)]
    sibling = (z * 2 + 1 - c, y, x)
    x_to = [(r, y, (x + d) % NX) for d in range(1, NX)]
    peers = y_to + z_to + [sibling] + x_to

    barrier = pltpu.get_barrier_semaphore()
    for peer in peers:
        pl.semaphore_signal(barrier, inc=1, device_id=peer, device_id_type=MESH)

    def spans(q):
        for i in range(SIDE // BW):
            lo, hi = max(STARTS[q], i * BW), min(STARTS[q] + PIECES[q], (i + 1) * BW)
            if lo < hi:
                yield i, lo, hi - lo

    loads = [
        pltpu.make_async_copy(slab.at[pl.ds(STARTS[q], n)], a_raw.at[pl.ds(STARTS[q], n)], ld_sem.at[q])
        for q, n in enumerate(PIECES)
    ] + [pltpu.make_async_copy(inner, b_raw, ld_sem.at[Q])]
    for i in [0, Q] + list(range(1, Q)):
        loads[i].start()

    def mask_slab(q):
        loads[q].wait()
        for i, lo, n in spans(q):
            for j in range(SIDE // BW):
                keep = slab_pat[i, 0, j].astype(jnp.float32).astype(jnp.bfloat16)
                at = (pl.ds(lo, n), pl.ds(j * BW, BW))
                a_all[(y, *at)] = a_raw[at] * keep

    def mask_inner():
        loads[Q].wait()
        for j in range(SIDE // BW):
            keep = inner_pat[0, 0, j].astype(jnp.float32).astype(jnp.bfloat16)
            cols = pl.ds(j * BW, BW)
            b_all[z, pl.ds(c * BW, BW), cols] = b_raw[:, cols] * keep

    def source(me, size, way, d):
        return (me + size - d) % size if way == 0 else (me + d) % size

    sends = []

    def start(copy):
        copy.start()
        sends.append(copy)

    def slab_copy(way, q, d, hop):
        n = PIECES[q] if hop < 3 else PIECES[q] // 2
        lo = STARTS[q] + (way * n if hop == 3 else 0)
        ref = a_all.at[source(y, NY, way, d), pl.ds(lo, n)]
        return pltpu.make_async_remote_copy(
            src_ref=ref, dst_ref=ref, send_sem=as_sem.at[way, q, hop], recv_sem=ar_sem.at[way, q, hop],
            device_id=y_to[way], device_id_type=MESH)

    def inner_ref(p, way, d, core, half):
        n = BP // 2 if half else BP
        lo = core * BW + p * BP + (way * n if half else 0)
        return b_all.at[source(z, NZ, way, d), pl.ds(lo, n)]

    def inner_copy(p, way, d, hop):
        ref = inner_ref(p, way, d, c, hop == 3)
        return pltpu.make_async_remote_copy(
            src_ref=ref, dst_ref=ref, send_sem=bs_sem.at[p, way, hop], recv_sem=br_sem.at[p, way, hop],
            device_id=z_to[way], device_id_type=MESH)

    def core_copy(p, way, d, core):
        ref = inner_ref(p, way, d, core, d == 4)
        return pltpu.make_async_remote_copy(
            src_ref=ref, dst_ref=ref, send_sem=ss_sem.at[p, way, d], recv_sem=sr_sem.at[p, way, d],
            device_id=sibling, device_id_type=MESH)

    def part_copy(q, d):
        rows = pl.ds(STARTS[q], PIECES[q])
        return pltpu.make_async_remote_copy(
            src_ref=acc.at[(x + d) % NX, rows], dst_ref=rs.at[d - 1, rows],
            send_sem=cs_sem.at[q, d - 1], recv_sem=cr_sem.at[q, d - 1],
            device_id=x_to[d - 1], device_id_type=MESH)

    def send_slab(q):
        mask_slab(q)
        for way in range(2):
            start(slab_copy(way, q, 0, 0))

    def send_inner():
        mask_inner()
        for p in range(PB):
            for way in range(2):
                start(inner_copy(p, way, 0, 0))
        for p in range(PB):
            start(core_copy(p, 0, 0, c))

    def pass_slab(q, d):
        for way in range(2):
            slab_copy(way, q, d, d - 1).wait_recv()
            if d < 4:
                start(slab_copy(way, q, d, d))

    def pass_inner(p, d):
        for way in range(2):
            inner_copy(p, way, d, d - 1).wait_recv()
            if d < 4:
                start(inner_copy(p, way, d, d))
            start(core_copy(p, way, d, c))

    def wait_core():
        for d in range(5):
            for way in range(2 if d else 1):
                for p in range(PB):
                    core_copy(p, way, d, 1 - c).wait_recv()

    def multiply(q0, nq, d):
        rows = pl.ds(STARTS[q0], sum(PIECES[q0:q0 + nq]))
        for way in range(2 if 0 < d < 4 else 1):
            src = source(y, NY, way, d)
            product = jnp.dot(a_all[src, rows, :], b_all[src], preferred_element_type=jnp.float32)
            for k in range(NX):
                part = product[:, k * 128:(k + 1) * 128]
                acc[k, rows] = part if d == 0 else acc[k, rows] + part

    def send_parts(q):
        for d in (2, 1, 3):
            start(part_copy(q, d))

    def finish(q):
        for d in range(1, NX):
            part_copy(q, d).wait_recv()
        for i, lo, n in spans(q):
            rows = pl.ds(lo, n)
            total = acc[x, rows] + rs[0, rows] + rs[1, rows] + rs[2, rows]
            keep = col_ids[x // 2] >= row_ids[i]
            out[rows, :] = jnp.where(keep, total, 0.0).astype(jnp.bfloat16)

    mask_slab(0)
    pl.semaphore_wait(barrier, len(peers))
    for way in range(2):
        start(slab_copy(way, 0, 0, 0))
    send_slab(1)
    send_inner()
    send_slab(2)
    send_slab(3)
    pass_slab(0, 1)
    pass_inner(0, 1)
    pass_slab(1, 1)
    pass_inner(1, 1)
    pass_slab(2, 1)
    pass_inner(0, 2)
    pass_slab(3, 1)
    pass_inner(1, 2)
    pass_slab(0, 2)
    pass_inner(0, 3)
    pass_slab(1, 2)
    pass_inner(1, 3)
    pass_inner(0, 4)
    pass_inner(1, 4)
    pass_slab(2, 2)
    pass_slab(3, 2)
    wait_core()
    for d in range(3):
        multiply(0, 2, d)
    pass_slab(0, 3)
    multiply(0, 1, 3)
    pass_slab(1, 3)
    multiply(1, 1, 3)
    for d in range(3):
        multiply(2, 2, d)
    pass_slab(0, 4)
    multiply(0, 1, 4)
    send_parts(0)
    pass_slab(2, 3)
    multiply(2, 1, 3)
    pass_slab(1, 4)
    multiply(1, 1, 4)
    send_parts(1)
    pass_slab(3, 3)
    multiply(3, 1, 3)
    pass_slab(2, 4)
    multiply(2, 1, 4)
    send_parts(2)
    pass_slab(3, 4)
    multiply(3, 1, 4)
    send_parts(3)
    for q in range(Q - 1):
        finish(q)
    for copy in sends:
        copy.wait_send()
    finish(Q - 1)


def on_device(slab_panel, slab_pattern, inner_panel, inner_pattern, slab_rows, column_ids):
    whole = pl.BlockSpec(memory_space=pl.ANY)
    scalars = pl.BlockSpec(memory_space=pltpu.SMEM)
    dma = pltpu.SemaphoreType.DMA
    return pl.pallas_call(
        kernel,
        out_shape=jax.ShapeDtypeStruct((SIDE, 128), jnp.bfloat16),
        in_specs=[whole, scalars, whole, scalars, scalars, scalars],
        out_specs=pl.BlockSpec(memory_space=pltpu.VMEM),
        scratch_shapes=[
            pltpu.VMEM((SIDE, SIDE), jnp.bfloat16),
            pltpu.VMEM((BW, SIDE), jnp.bfloat16),
            pltpu.VMEM((NY, SIDE, SIDE), jnp.bfloat16),
            pltpu.VMEM((NZ, SIDE, SIDE), jnp.bfloat16),
            pltpu.VMEM((NX, SIDE, 128), jnp.float32),
            pltpu.VMEM((NX - 1, SIDE, 128), jnp.float32),
            dma((Q + 1,)),
            dma((2, Q, 4)), dma((2, Q, 4)),
            dma((PB, 2, 4)), dma((PB, 2, 4)),
            dma((PB, 2, 5)), dma((PB, 2, 5)),
            dma((Q, NX - 1)), dma((Q, NX - 1)),
        ],
        compiler_params=pltpu.CompilerParams(
            collective_id=0, has_side_effects=True, vmem_limit_bytes=60 * 1024 * 1024),
    )(slab_panel.reshape(SIDE, SIDE), slab_pattern, inner_panel.reshape(BW, SIDE), inner_pattern,
      slab_rows, column_ids)


def solution(mesh):
    return jax.shard_map(
        on_device,
        mesh=mesh,
        in_specs=(
            P("row", "layer", "col"),
            P("row", "layer", "col"),
            P("layer", "row", "col"),
            P("layer", "row", "col"),
            P("row"),
            P("col"),
        ),
        out_specs=P("row", ("col", "layer")),
        check_vma=False,
    )
```

```python
import jax
import jax.numpy as jnp
from jax import lax
from jax.experimental import pallas as pl
from jax.experimental.pallas import tpu as pltpu
from jax.sharding import PartitionSpec as P

MESH = pl.DeviceIdType.MESH
BW = 256
NY, NZ, NX = 8, 8, 4
SIDE = 512
PIECES = (128, 128, 128, 128)
STARTS = tuple(sum(PIECES[:q]) for q in range(len(PIECES)))
Q = len(PIECES)
PB = 2
BP = BW // PB


def kernel(slab, slab_pat, inner, inner_pat, row_ids, col_ids, out,
           a_raw, b_raw, a_all, b_all, acc, rs,
           ld_sem, as_sem, ar_sem, bs_sem, br_sem, ss_sem, sr_sem, cs_sem, cr_sem):
    r, y, x = lax.axis_index("row"), lax.axis_index("col"), lax.axis_index("layer")
    z, c = r // 2, r % 2
    y_to = [(r, (y + 1) % NY, x), (r, (y + NY - 1) % NY, x)]
    z_to = [(((z + 1) % NZ) * 2 + c, y, x), (((z + NZ - 1) % NZ) * 2 + c, y, x)]
    sibling = (z * 2 + 1 - c, y, x)
    x_to = [(r, y, (x + d) % NX) for d in range(1, NX)]
    peers = y_to + z_to + [sibling] + x_to

    barrier = pltpu.get_barrier_semaphore()
    for peer in peers:
        pl.semaphore_signal(barrier, inc=1, device_id=peer, device_id_type=MESH)

    def spans(q):
        for i in range(SIDE // BW):
            lo, hi = max(STARTS[q], i * BW), min(STARTS[q] + PIECES[q], (i + 1) * BW)
            if lo < hi:
                yield i, lo, hi - lo

    loads = [
        pltpu.make_async_copy(slab.at[pl.ds(STARTS[q], n)], a_raw.at[pl.ds(STARTS[q], n)], ld_sem.at[q])
        for q, n in enumerate(PIECES)
    ] + [pltpu.make_async_copy(inner, b_raw, ld_sem.at[Q])]
    for i in [0, Q] + list(range(1, Q)):
        loads[i].start()

    def mask_slab(q):
        loads[q].wait()
        for i, lo, n in spans(q):
            for j in range(SIDE // BW):
                keep = slab_pat[i, 0, j].astype(jnp.float32).astype(jnp.bfloat16)
                at = (pl.ds(lo, n), pl.ds(j * BW, BW))
                a_all[(y, *at)] = a_raw[at] * keep

    def mask_inner():
        loads[Q].wait()
        for j in range(SIDE // BW):
            keep = inner_pat[0, 0, j].astype(jnp.float32).astype(jnp.bfloat16)
            cols = pl.ds(j * BW, BW)
            b_all[z, pl.ds(c * BW, BW), cols] = b_raw[:, cols] * keep

    def source(me, size, way, d):
        return (me + size - d) % size if way == 0 else (me + d) % size

    sends = []

    def start(copy):
        copy.start()
        sends.append(copy)

    def slab_copy(way, q, d, hop):
        n = PIECES[q] if hop < 3 else PIECES[q] // 2
        lo = STARTS[q] + (way * n if hop == 3 else 0)
        ref = a_all.at[source(y, NY, way, d), pl.ds(lo, n)]
        return pltpu.make_async_remote_copy(
            src_ref=ref, dst_ref=ref, send_sem=as_sem.at[way, q, hop], recv_sem=ar_sem.at[way, q, hop],
            device_id=y_to[way], device_id_type=MESH)

    def inner_ref(p, way, d, core, half):
        n = BP // 2 if half else BP
        lo = core * BW + p * BP + (way * n if half else 0)
        return b_all.at[source(z, NZ, way, d), pl.ds(lo, n)]

    def inner_copy(p, way, d, hop):
        ref = inner_ref(p, way, d, c, hop == 3)
        return pltpu.make_async_remote_copy(
            src_ref=ref, dst_ref=ref, send_sem=bs_sem.at[p, way, hop], recv_sem=br_sem.at[p, way, hop],
            device_id=z_to[way], device_id_type=MESH)

    def core_copy(p, way, d, core):
        ref = inner_ref(p, way, d, core, d == 4)
        return pltpu.make_async_remote_copy(
            src_ref=ref, dst_ref=ref, send_sem=ss_sem.at[p, way, d], recv_sem=sr_sem.at[p, way, d],
            device_id=sibling, device_id_type=MESH)

    def part_copy(q, d):
        rows = pl.ds(STARTS[q], PIECES[q])
        return pltpu.make_async_remote_copy(
            src_ref=acc.at[(x + d) % NX, rows], dst_ref=rs.at[d - 1, rows],
            send_sem=cs_sem.at[q, d - 1], recv_sem=cr_sem.at[q, d - 1],
            device_id=x_to[d - 1], device_id_type=MESH)

    def send_slab(q):
        mask_slab(q)
        for way in range(2):
            start(slab_copy(way, q, 0, 0))

    def send_inner():
        mask_inner()
        for p in range(PB):
            for way in range(2):
                start(inner_copy(p, way, 0, 0))
        for p in range(PB):
            start(core_copy(p, 0, 0, c))

    def pass_slab(q, d):
        for way in range(2):
            slab_copy(way, q, d, d - 1).wait_recv()
            if d < 4:
                start(slab_copy(way, q, d, d))

    def pass_inner(p, d):
        for way in range(2):
            inner_copy(p, way, d, d - 1).wait_recv()
            if d < 4:
                start(inner_copy(p, way, d, d))
            start(core_copy(p, way, d, c))

    def wait_core():
        for d in range(5):
            for way in range(2 if d else 1):
                for p in range(PB):
                    core_copy(p, way, d, 1 - c).wait_recv()

    def multiply(q0, nq, d):
        rows = pl.ds(STARTS[q0], sum(PIECES[q0:q0 + nq]))
        for way in range(2 if 0 < d < 4 else 1):
            src = source(y, NY, way, d)
            product = jnp.dot(a_all[src, rows, :], b_all[src], preferred_element_type=jnp.float32)
            for k in range(NX):
                part = product[:, k * 128:(k + 1) * 128]
                acc[k, rows] = part if d == 0 else acc[k, rows] + part

    def send_parts(q):
        for d in (2, 1, 3):
            start(part_copy(q, d))

    def finish(q):
        for d in range(1, NX):
            part_copy(q, d).wait_recv()
        for i, lo, n in spans(q):
            rows = pl.ds(lo, n)
            total = acc[x, rows] + rs[0, rows] + rs[1, rows] + rs[2, rows]
            keep = col_ids[x // 2] >= row_ids[i]
            out[rows, :] = jnp.where(keep, total, 0.0).astype(jnp.bfloat16)

    mask_slab(0)
    pl.semaphore_wait(barrier, len(peers))
    for way in range(2):
        start(slab_copy(way, 0, 0, 0))
    send_slab(1)
    send_inner()
    send_slab(2)
    send_slab(3)
    pass_slab(0, 1)
    pass_inner(0, 1)
    pass_slab(1, 1)
    pass_inner(1, 1)
    pass_slab(2, 1)
    pass_inner(0, 2)
    pass_slab(3, 1)
    pass_inner(1, 2)
    pass_slab(0, 2)
    pass_inner(0, 3)
    pass_slab(1, 2)
    pass_inner(1, 3)
    pass_inner(0, 4)
    pass_inner(1, 4)
    pass_slab(2, 2)
    pass_slab(3, 2)
    wait_core()
    for d in range(3):
        multiply(0, 2, d)
    pass_slab(0, 3)
    multiply(0, 1, 3)
    pass_slab(1, 3)
    multiply(1, 1, 3)
    for d in range(3):
        multiply(2, 2, d)
    pass_slab(0, 4)
    multiply(0, 1, 4)
    send_parts(0)
    pass_slab(2, 3)
    multiply(2, 1, 3)
    pass_slab(1, 4)
    multiply(1, 1, 4)
    send_parts(1)
    pass_slab(3, 3)
    multiply(3, 1, 3)
    pass_slab(2, 4)
    multiply(2, 1, 4)
    send_parts(2)
    pass_slab(3, 4)
    multiply(3, 1, 4)
    send_parts(3)
    for q in range(Q - 1):
        finish(q)
    for copy in sends:
        copy.wait_send()
    finish(Q - 1)


def on_device(slab_panel, slab_pattern, inner_panel, inner_pattern, slab_rows, column_ids):
    whole = pl.BlockSpec(memory_space=pl.ANY)
    scalars = pl.BlockSpec(memory_space=pltpu.SMEM)
    dma = pltpu.SemaphoreType.DMA
    return pl.pallas_call(
        kernel,
        out_shape=jax.ShapeDtypeStruct((SIDE, 128), jnp.bfloat16),
        in_specs=[whole, scalars, whole, scalars, scalars, scalars],
        out_specs=pl.BlockSpec(memory_space=pltpu.VMEM),
        scratch_shapes=[
            pltpu.VMEM((SIDE, SIDE), jnp.bfloat16),
            pltpu.VMEM((BW, SIDE), jnp.bfloat16),
            pltpu.VMEM((NY, SIDE, SIDE), jnp.bfloat16),
            pltpu.VMEM((NZ, SIDE, SIDE), jnp.bfloat16),
            pltpu.VMEM((NX, SIDE, 128), jnp.float32),
            pltpu.VMEM((NX - 1, SIDE, 128), jnp.float32),
            dma((Q + 1,)),
            dma((2, Q, 4)), dma((2, Q, 4)),
            dma((PB, 2, 4)), dma((PB, 2, 4)),
            dma((PB, 2, 5)), dma((PB, 2, 5)),
            dma((Q, NX - 1)), dma((Q, NX - 1)),
        ],
        compiler_params=pltpu.CompilerParams(
            collective_id=0, has_side_effects=True, vmem_limit_bytes=54976 * 1024),
    )(slab_panel.reshape(SIDE, SIDE), slab_pattern, inner_panel.reshape(BW, SIDE), inner_pattern,
      slab_rows, column_ids)


def solution(mesh):
    return jax.shard_map(
        on_device,
        mesh=mesh,
        in_specs=(
            P("row", "layer", "col"),
            P("row", "layer", "col"),
            P("layer", "row", "col"),
            P("layer", "row", "col"),
            P("row"),
            P("col"),
        ),
        out_specs=P("row", ("col", "layer")),
        check_vma=False,
    )
```

```python
import jax
import jax.numpy as jnp
from jax import lax
from jax.experimental import pallas as pl
from jax.experimental.pallas import tpu as pltpu
from jax.sharding import PartitionSpec as P

MESH = pl.DeviceIdType.MESH
BW = 256
NY, NZ, NX = 8, 8, 4
SIDE = 512
PIECES = (128, 128, 128, 128)
STARTS = tuple(sum(PIECES[:q]) for q in range(len(PIECES)))
Q = len(PIECES)
PB = 2
BP = BW // PB

FINISH = (
    ("slab", 0, 4), ("multiply", 0, 1, 4), ("parts", 0),
    ("slab", 2, 3), ("multiply", 2, 1, 3),
    ("slab", 1, 4), ("multiply", 1, 1, 4), ("parts", 1),
    ("slab", 3, 3), ("multiply", 3, 1, 3),
    ("slab", 2, 4), ("multiply", 2, 1, 4), ("parts", 2),
    ("slab", 3, 4), ("multiply", 3, 1, 4), ("parts", 3),
    ("finish", 0), ("finish", 1), ("finish", 2), ("end",), ("finish", 3),
)
OTHER_PLANES = (
    ("enter",), ("first_slab",), ("send_slab", 1), ("send_inner",), ("send_slab", 2), ("send_slab", 3),
    ("slab", 0, 1), ("inner", 0, 1), ("slab", 1, 1), ("inner", 1, 1),
    ("slab", 2, 1), ("inner", 0, 2), ("slab", 3, 1), ("inner", 1, 2),
    ("slab", 0, 2), ("inner", 0, 3), ("slab", 1, 2), ("inner", 1, 3),
    ("inner", 0, 4), ("inner", 1, 4), ("slab", 2, 2), ("slab", 3, 2), ("wait_core",),
    ("multiply", 0, 2, 0), ("multiply", 0, 2, 1), ("multiply", 0, 2, 2),
    ("slab", 0, 3), ("multiply", 0, 1, 3), ("slab", 1, 3), ("multiply", 1, 1, 3),
    ("multiply", 2, 2, 0), ("multiply", 2, 2, 1), ("multiply", 2, 2, 2),
) + FINISH
FIRST_PLANE = (
    ("enter_first",), ("first_slab",), ("send_slab", 1), ("send_slab", 2), ("send_slab", 3),
    ("slab", 0, 1), ("meet",), ("send_inner",), ("slab", 1, 1), ("slab", 2, 1), ("slab", 3, 1),
    ("inner", 0, 1), ("slab", 0, 2), ("inner", 1, 1), ("slab", 1, 2), ("inner", 0, 2), ("inner", 1, 2),
    ("slab", 2, 2), ("slab", 3, 2), ("inner", 0, 3), ("slab", 0, 3), ("inner", 1, 3),
    ("inner", 0, 4), ("slab", 1, 3), ("inner", 1, 4), ("wait_core",),
    ("multiply", 0, 4, 0), ("multiply", 0, 4, 1), ("multiply", 0, 4, 2), ("multiply", 0, 2, 3),
) + FINISH


def kernel(slab, slab_pat, inner, inner_pat, row_ids, col_ids, out,
           a_raw, b_raw, a_all, b_all, acc, rs,
           meet_sem, ld_sem, as_sem, ar_sem, bs_sem, br_sem, ss_sem, sr_sem, cs_sem, cr_sem):
    r, y, x = lax.axis_index("row"), lax.axis_index("col"), lax.axis_index("layer")
    z, c = r // 2, r % 2
    y_to = [(r, (y + 1) % NY, x), (r, (y + NY - 1) % NY, x)]
    z_to = [(((z + 1) % NZ) * 2 + c, y, x), (((z + NZ - 1) % NZ) * 2 + c, y, x)]
    sibling = (z * 2 + 1 - c, y, x)
    x_to = [(r, y, (x + d) % NX) for d in range(1, NX)]
    barrier = pltpu.get_barrier_semaphore()
    for peer in y_to + [sibling] + x_to:
        pl.semaphore_signal(barrier, inc=1, device_id=peer, device_id_type=MESH)
    near = len(y_to) + 1 + len(x_to)
    for step in (1, NZ - 1):
        @pl.when(jnp.logical_and(z != 0, (z + step) % NZ != 0))
        def _(step=step):
            pl.semaphore_signal(
                barrier, inc=1, device_id=(((z + step) % NZ) * 2 + c, y, x), device_id_type=MESH)

    def spans(q):
        for i in range(SIDE // BW):
            lo, hi = max(STARTS[q], i * BW), min(STARTS[q] + PIECES[q], (i + 1) * BW)
            if lo < hi:
                yield i, lo, hi - lo

    loads = [
        pltpu.make_async_copy(slab.at[pl.ds(STARTS[q], n)], a_raw.at[pl.ds(STARTS[q], n)], ld_sem.at[q])
        for q, n in enumerate(PIECES)
    ] + [pltpu.make_async_copy(inner, b_raw, ld_sem.at[Q])]
    for i in [0, Q] + list(range(1, Q)):
        loads[i].start()

    def mask_slab(q):
        loads[q].wait()
        for i, lo, n in spans(q):
            for j in range(SIDE // BW):
                keep = slab_pat[i, 0, j].astype(jnp.float32).astype(jnp.bfloat16)
                at = (pl.ds(lo, n), pl.ds(j * BW, BW))
                a_all[(y, *at)] = a_raw[at] * keep

    def mask_inner():
        loads[Q].wait()
        for j in range(SIDE // BW):
            keep = inner_pat[0, 0, j].astype(jnp.float32).astype(jnp.bfloat16)
            cols = pl.ds(j * BW, BW)
            b_all[z, pl.ds(c * BW, BW), cols] = b_raw[:, cols] * keep

    def source(me, size, way, d):
        return (me + size - d) % size if way == 0 else (me + d) % size

    sends = []

    def start(copy):
        copy.start()
        sends.append(copy)

    def slab_copy(way, q, d, hop):
        n = PIECES[q] if hop < 3 else PIECES[q] // 2
        lo = STARTS[q] + (way * n if hop == 3 else 0)
        ref = a_all.at[source(y, NY, way, d), pl.ds(lo, n)]
        return pltpu.make_async_remote_copy(
            src_ref=ref, dst_ref=ref, send_sem=as_sem.at[way, q, hop], recv_sem=ar_sem.at[way, q, hop],
            device_id=y_to[way], device_id_type=MESH)

    def inner_ref(p, way, d, core, half):
        n = BP // 2 if half else BP
        lo = core * BW + p * BP + (way * n if half else 0)
        return b_all.at[source(z, NZ, way, d), pl.ds(lo, n)]

    def inner_copy(p, way, d, hop):
        ref = inner_ref(p, way, d, c, hop == 3)
        return pltpu.make_async_remote_copy(
            src_ref=ref, dst_ref=ref, send_sem=bs_sem.at[p, way, hop], recv_sem=br_sem.at[p, way, hop],
            device_id=z_to[way], device_id_type=MESH)

    def core_copy(p, way, d, core):
        ref = inner_ref(p, way, d, core, d == 4)
        return pltpu.make_async_remote_copy(
            src_ref=ref, dst_ref=ref, send_sem=ss_sem.at[p, way, d], recv_sem=sr_sem.at[p, way, d],
            device_id=sibling, device_id_type=MESH)

    def part_copy(q, d):
        rows = pl.ds(STARTS[q], PIECES[q])
        return pltpu.make_async_remote_copy(
            src_ref=acc.at[(x + d) % NX, rows], dst_ref=rs.at[d - 1, rows],
            send_sem=cs_sem.at[q, d - 1], recv_sem=cr_sem.at[q, d - 1],
            device_id=x_to[d - 1], device_id_type=MESH)

    def send_slab(q):
        mask_slab(q)
        for way in range(2):
            start(slab_copy(way, q, 0, 0))

    def send_inner():
        mask_inner()
        for p in range(PB):
            for way in range(2):
                start(inner_copy(p, way, 0, 0))
        for p in range(PB):
            start(core_copy(p, 0, 0, c))

    def pass_slab(q, d):
        for way in range(2):
            slab_copy(way, q, d, d - 1).wait_recv()
            if d < 4:
                start(slab_copy(way, q, d, d))

    def pass_inner(p, d):
        for way in range(2):
            inner_copy(p, way, d, d - 1).wait_recv()
            if d < 4:
                start(inner_copy(p, way, d, d))
            start(core_copy(p, way, d, c))

    def wait_core():
        for d in range(5):
            for way in range(2 if d else 1):
                for p in range(PB):
                    core_copy(p, way, d, 1 - c).wait_recv()

    def multiply(q0, nq, d):
        rows = pl.ds(STARTS[q0], sum(PIECES[q0:q0 + nq]))
        for way in range(2 if 0 < d < 4 else 1):
            src = source(y, NY, way, d)
            product = jnp.dot(a_all[src, rows, :], b_all[src], preferred_element_type=jnp.float32)
            for k in range(NX):
                part = product[:, k * 128:(k + 1) * 128]
                acc[k, rows] = part if d == 0 else acc[k, rows] + part

    def send_parts(q):
        for d in (2, 1, 3):
            start(part_copy(q, d))

    def finish(q):
        for d in range(1, NX):
            part_copy(q, d).wait_recv()
        for i, lo, n in spans(q):
            rows = pl.ds(lo, n)
            total = acc[x, rows] + rs[0, rows] + rs[1, rows] + rs[2, rows]
            keep = col_ids[x // 2] >= row_ids[i]
            out[rows, :] = jnp.where(keep, total, 0.0).astype(jnp.bfloat16)

    def end():
        for copy in sends:
            copy.wait_send()

    def enter_first():
        mask_slab(0)
        pl.semaphore_wait(barrier, near)
        for peer in z_to:
            pl.semaphore_signal(barrier, inc=1, device_id=peer, device_id_type=MESH)

    def enter():
        mask_slab(0)
        pl.semaphore_wait(barrier, near + 2)

        for step in (1, NZ - 1):
            @pl.when((z + step) % NZ == 0)
            def _(step=step):
                pl.semaphore_signal(
                    meet_sem, inc=1, device_id=(((z + step) % NZ) * 2 + c, y, x), device_id_type=MESH)

    def meet():
        pl.semaphore_wait(meet_sem, 2)

    def first_slab():
        for way in range(2):
            start(slab_copy(way, 0, 0, 0))

    steps = {
        "enter_first": enter_first, "enter": enter, "meet": meet, "first_slab": first_slab,
        "send_slab": send_slab, "send_inner": send_inner, "slab": pass_slab, "inner": pass_inner,
        "wait_core": wait_core, "multiply": multiply, "parts": send_parts, "finish": finish, "end": end,
    }

    def run(schedule):
        sends.clear()
        for name, *args in schedule:
            steps[name](*args)

    pl.when(z == 0)(lambda: run(FIRST_PLANE))
    pl.when(z != 0)(lambda: run(OTHER_PLANES))


def on_device(slab_panel, slab_pattern, inner_panel, inner_pattern, slab_rows, column_ids):
    whole = pl.BlockSpec(memory_space=pl.ANY)
    scalars = pl.BlockSpec(memory_space=pltpu.SMEM)
    dma = pltpu.SemaphoreType.DMA
    return pl.pallas_call(
        kernel,
        out_shape=jax.ShapeDtypeStruct((SIDE, 128), jnp.bfloat16),
        in_specs=[whole, scalars, whole, scalars, scalars, scalars],
        out_specs=pl.BlockSpec(memory_space=pltpu.VMEM),
        scratch_shapes=[
            pltpu.VMEM((SIDE, SIDE), jnp.bfloat16),
            pltpu.VMEM((BW, SIDE), jnp.bfloat16),
            pltpu.VMEM((NY, SIDE, SIDE), jnp.bfloat16),
            pltpu.VMEM((NZ, SIDE, SIDE), jnp.bfloat16),
            pltpu.VMEM((NX, SIDE, 128), jnp.float32),
            pltpu.VMEM((NX - 1, SIDE, 128), jnp.float32),
            pltpu.SemaphoreType.REGULAR,
            dma((Q + 1,)),
            dma((2, Q, 4)), dma((2, Q, 4)),
            dma((PB, 2, 4)), dma((PB, 2, 4)),
            dma((PB, 2, 5)), dma((PB, 2, 5)),
            dma((Q, NX - 1)), dma((Q, NX - 1)),
        ],
        compiler_params=pltpu.CompilerParams(
            collective_id=0, has_side_effects=True, vmem_limit_bytes=54976 * 1024),
    )(slab_panel.reshape(SIDE, SIDE), slab_pattern, inner_panel.reshape(BW, SIDE), inner_pattern,
      slab_rows, column_ids)


def solution(mesh):
    return jax.shard_map(
        on_device,
        mesh=mesh,
        in_specs=(
            P("row", "layer", "col"),
            P("row", "layer", "col"),
            P("layer", "row", "col"),
            P("layer", "row", "col"),
            P("row"),
            P("col"),
        ),
        out_specs=P("row", ("col", "layer")),
        check_vma=False,
    )
```

```python
import jax
import jax.numpy as jnp
from jax import lax
from jax.experimental import pallas as pl
from jax.experimental.pallas import tpu as pltpu
from jax.sharding import PartitionSpec as P

MESH = pl.DeviceIdType.MESH
BW = 256
NY, NZ, NX = 8, 8, 4
SIDE = 512
PIECES = (128, 128, 128, 128)
STARTS = tuple(sum(PIECES[:q]) for q in range(len(PIECES)))
Q = len(PIECES)
PB = 2
BP = BW // PB

FINISH = (
    ("slab", 0, 4), ("multiply", 0, 1, 4), ("meet", "x"), ("parts", 0),
    ("slab", 2, 3), ("multiply", 2, 1, 3),
    ("slab", 1, 4), ("multiply", 1, 1, 4), ("parts", 1),
    ("slab", 3, 3), ("multiply", 3, 1, 3),
    ("slab", 2, 4), ("multiply", 2, 1, 4), ("parts", 2),
    ("slab", 3, 4), ("multiply", 3, 1, 4), ("parts", 3),
    ("finish", 0), ("finish", 1), ("finish", 2), ("end",), ("finish", 3),
)
OTHER_PLANES = (
    ("first_slab",), ("send_slab", 1), ("send_inner",), ("send_slab", 2), ("send_slab", 3),
    ("share_inner",), ("slab", 0, 1), ("inner", 0, 1), ("slab", 1, 1), ("inner", 1, 1),
    ("slab", 2, 1), ("inner", 0, 2), ("slab", 3, 1), ("inner", 1, 2),
    ("slab", 0, 2), ("inner", 0, 3), ("slab", 1, 2), ("inner", 1, 3),
    ("inner", 0, 4), ("inner", 1, 4), ("slab", 2, 2), ("slab", 3, 2), ("wait_core",),
    ("multiply", 0, 2, 0), ("multiply", 0, 2, 1), ("multiply", 0, 2, 2),
    ("slab", 0, 3), ("multiply", 0, 1, 3), ("slab", 1, 3), ("multiply", 1, 1, 3),
    ("multiply", 2, 2, 0), ("multiply", 2, 2, 1), ("multiply", 2, 2, 2),
) + FINISH
FIRST_PLANE = (
    ("first_slab",), ("send_slab", 1), ("send_slab", 2), ("send_slab", 3), ("slab", 0, 1), ("send_inner",),
    ("share_inner",), ("slab", 1, 1), ("slab", 2, 1), ("inner", 0, 1), ("slab", 3, 1), ("inner", 1, 1),
    ("slab", 0, 2), ("inner", 0, 2), ("slab", 1, 2), ("inner", 1, 2), ("slab", 2, 2), ("inner", 0, 3),
    ("slab", 3, 2), ("inner", 1, 3), ("slab", 0, 3), ("inner", 0, 4), ("inner", 1, 4), ("slab", 1, 3),
    ("wait_core",), ("multiply", 0, 4, 0), ("multiply", 0, 4, 1), ("multiply", 0, 4, 2),
    ("multiply", 0, 2, 3),
) + FINISH


def kernel(slab, slab_pat, inner, inner_pat, row_ids, col_ids, out,
           a_raw, b_raw, a_all, b_all, acc, rs,
           meet_sem, ld_sem, as_sem, ar_sem, bs_sem, br_sem, ss_sem, sr_sem, cs_sem, cr_sem):
    r, y, x = lax.axis_index("row"), lax.axis_index("col"), lax.axis_index("layer")
    z, c = r // 2, r % 2
    y_to = [(r, (y + 1) % NY, x), (r, (y + NY - 1) % NY, x)]
    z_to = [(((z + 1) % NZ) * 2 + c, y, x), (((z + NZ - 1) % NZ) * 2 + c, y, x)]
    sibling = (z * 2 + 1 - c, y, x)
    x_to = [(r, y, (x + d) % NX) for d in range(1, NX)]
    gray = (0, 1, 3, 2)

    def before(a, b, order):
        less = [jnp.logical_and(a == i, b == k) for i in range(len(order)) for k in range(len(order))
                if order[i] < order[k]]
        out = less[0]
        for term in less[1:]:
            out = jnp.logical_or(out, term)
        return out

    z_rank = gray + tuple(range(4, NZ))
    pairs = {
        "core": [(sibling, c == 0)],
        "x": [(peer, before(x, (x + d) % NX, gray)) for d, peer in enumerate(x_to, 1)],
        "up": [(z_to[0], before(z, (z + 1) % NZ, z_rank))],
        "down": [(z_to[1], before(z, (z + NZ - 1) % NZ, z_rank))],
    }
    answer = {"core": meet_sem.at[0], "x": meet_sem.at[1], "up": meet_sem.at[3], "down": meet_sem.at[2]}
    mine = {"core": meet_sem.at[0], "x": meet_sem.at[1], "up": meet_sem.at[2], "down": meet_sem.at[3]}

    def signal(sem, peer):
        pl.semaphore_signal(sem, inc=1, device_id=peer, device_id_type=MESH)

    barrier = pltpu.get_barrier_semaphore()
    for peer in y_to:
        signal(barrier, peer)
    for kind in pairs:
        for peer, first in pairs[kind]:
            pl.when(first)(lambda peer=peer: signal(barrier, peer))

    def count(flags):
        return sum(jnp.where(flag, 1, 0) for flag in flags)

    def enter():
        seconds = [jnp.logical_not(first) for kind in pairs for _, first in pairs[kind]]
        pl.semaphore_wait(barrier, len(y_to) + count(seconds))

    def reply():
        for kind in pairs:
            for peer, first in pairs[kind]:
                pl.when(jnp.logical_not(first))(lambda kind=kind, peer=peer: signal(answer[kind], peer))

    def meet(kind):
        firsts = count([first for _, first in pairs[kind]])
        pl.when(firsts > 0)(lambda: pl.semaphore_wait(mine[kind], firsts))

    def spans(q):
        for i in range(SIDE // BW):
            lo, hi = max(STARTS[q], i * BW), min(STARTS[q] + PIECES[q], (i + 1) * BW)
            if lo < hi:
                yield i, lo, hi - lo

    loads = [
        pltpu.make_async_copy(slab.at[pl.ds(STARTS[q], n)], a_raw.at[pl.ds(STARTS[q], n)], ld_sem.at[q])
        for q, n in enumerate(PIECES)
    ] + [pltpu.make_async_copy(inner, b_raw, ld_sem.at[Q])]
    for i in [0, Q] + list(range(1, Q)):
        loads[i].start()

    def mask_slab(q):
        loads[q].wait()
        for i, lo, n in spans(q):
            for j in range(SIDE // BW):
                keep = slab_pat[i, 0, j].astype(jnp.float32).astype(jnp.bfloat16)
                at = (pl.ds(lo, n), pl.ds(j * BW, BW))
                a_all[(y, *at)] = a_raw[at] * keep

    def mask_inner():
        loads[Q].wait()
        for j in range(SIDE // BW):
            keep = inner_pat[0, 0, j].astype(jnp.float32).astype(jnp.bfloat16)
            cols = pl.ds(j * BW, BW)
            b_all[z, pl.ds(c * BW, BW), cols] = b_raw[:, cols] * keep

    def source(me, size, way, d):
        return (me + size - d) % size if way == 0 else (me + d) % size

    sends = []

    def start(copy):
        copy.start()
        sends.append(copy)

    def slab_copy(way, q, d, hop):
        n = PIECES[q] if hop < 3 else PIECES[q] // 2
        lo = STARTS[q] + (way * n if hop == 3 else 0)
        ref = a_all.at[source(y, NY, way, d), pl.ds(lo, n)]
        return pltpu.make_async_remote_copy(
            src_ref=ref, dst_ref=ref, send_sem=as_sem.at[way, q, hop], recv_sem=ar_sem.at[way, q, hop],
            device_id=y_to[way], device_id_type=MESH)

    def inner_ref(p, way, d, core, half):
        n = BP // 2 if half else BP
        lo = core * BW + p * BP + (way * n if half else 0)
        return b_all.at[source(z, NZ, way, d), pl.ds(lo, n)]

    def inner_copy(p, way, d, hop):
        ref = inner_ref(p, way, d, c, hop == 3)
        return pltpu.make_async_remote_copy(
            src_ref=ref, dst_ref=ref, send_sem=bs_sem.at[p, way, hop], recv_sem=br_sem.at[p, way, hop],
            device_id=z_to[way], device_id_type=MESH)

    def core_copy(p, way, d, core):
        ref = inner_ref(p, way, d, core, d == 4)
        return pltpu.make_async_remote_copy(
            src_ref=ref, dst_ref=ref, send_sem=ss_sem.at[p, way, d], recv_sem=sr_sem.at[p, way, d],
            device_id=sibling, device_id_type=MESH)

    def part_copy(q, d):
        rows = pl.ds(STARTS[q], PIECES[q])
        return pltpu.make_async_remote_copy(
            src_ref=acc.at[(x + d) % NX, rows], dst_ref=rs.at[d - 1, rows],
            send_sem=cs_sem.at[q, d - 1], recv_sem=cr_sem.at[q, d - 1],
            device_id=x_to[d - 1], device_id_type=MESH)

    def send_slab(q):
        mask_slab(q)
        for way in range(2):
            start(slab_copy(way, q, 0, 0))

    def send_inner():
        mask_inner()
        for way, kind in enumerate(("up", "down")):
            meet(kind)
            for p in range(PB):
                start(inner_copy(p, way, 0, 0))

    def share_inner():
        meet("core")
        for p in range(PB):
            start(core_copy(p, 0, 0, c))

    def pass_slab(q, d):
        for way in range(2):
            slab_copy(way, q, d, d - 1).wait_recv()
            if d < 4:
                start(slab_copy(way, q, d, d))

    def pass_inner(p, d):
        for way in range(2):
            inner_copy(p, way, d, d - 1).wait_recv()
            if d < 4:
                start(inner_copy(p, way, d, d))
            start(core_copy(p, way, d, c))

    def wait_core():
        for d in range(5):
            for way in range(2 if d else 1):
                for p in range(PB):
                    core_copy(p, way, d, 1 - c).wait_recv()

    def multiply(q0, nq, d):
        rows = pl.ds(STARTS[q0], sum(PIECES[q0:q0 + nq]))
        for way in range(2 if 0 < d < 4 else 1):
            src = source(y, NY, way, d)
            product = jnp.dot(a_all[src, rows, :], b_all[src], preferred_element_type=jnp.float32)
            for k in range(NX):
                part = product[:, k * 128:(k + 1) * 128]
                acc[k, rows] = part if d == 0 else acc[k, rows] + part

    def send_parts(q):
        for d in (2, 1, 3):
            start(part_copy(q, d))

    def finish(q):
        for d in range(1, NX):
            part_copy(q, d).wait_recv()
        for i, lo, n in spans(q):
            rows = pl.ds(lo, n)
            total = acc[x, rows] + rs[0, rows] + rs[1, rows] + rs[2, rows]
            keep = col_ids[x // 2] >= row_ids[i]
            out[rows, :] = jnp.where(keep, total, 0.0).astype(jnp.bfloat16)

    def end():
        for copy in sends:
            copy.wait_send()

    def first_slab():
        mask_slab(0)
        enter()
        for way in range(2):
            start(slab_copy(way, 0, 0, 0))
        reply()

    steps = {
        "first_slab": first_slab, "meet": meet, "send_slab": send_slab, "send_inner": send_inner,
        "share_inner": share_inner, "slab": pass_slab, "inner": pass_inner,
        "wait_core": wait_core, "multiply": multiply, "parts": send_parts, "finish": finish, "end": end,
    }

    def run(schedule):
        sends.clear()
        for name, *args in schedule:
            steps[name](*args)

    pl.when(z == 0)(lambda: run(FIRST_PLANE))
    pl.when(z != 0)(lambda: run(OTHER_PLANES))


def on_device(slab_panel, slab_pattern, inner_panel, inner_pattern, slab_rows, column_ids):
    whole = pl.BlockSpec(memory_space=pl.ANY)
    scalars = pl.BlockSpec(memory_space=pltpu.SMEM)
    dma = pltpu.SemaphoreType.DMA
    return pl.pallas_call(
        kernel,
        out_shape=jax.ShapeDtypeStruct((SIDE, 128), jnp.bfloat16),
        in_specs=[whole, scalars, whole, scalars, scalars, scalars],
        out_specs=pl.BlockSpec(memory_space=pltpu.VMEM),
        scratch_shapes=[
            pltpu.VMEM((SIDE, SIDE), jnp.bfloat16),
            pltpu.VMEM((BW, SIDE), jnp.bfloat16),
            pltpu.VMEM((NY, SIDE, SIDE), jnp.bfloat16),
            pltpu.VMEM((NZ, SIDE, SIDE), jnp.bfloat16),
            pltpu.VMEM((NX, SIDE, 128), jnp.float32),
            pltpu.VMEM((NX - 1, SIDE, 128), jnp.float32),
            pltpu.SemaphoreType.REGULAR((4,)),
            dma((Q + 1,)),
            dma((2, Q, 4)), dma((2, Q, 4)),
            dma((PB, 2, 4)), dma((PB, 2, 4)),
            dma((PB, 2, 5)), dma((PB, 2, 5)),
            dma((Q, NX - 1)), dma((Q, NX - 1)),
        ],
        compiler_params=pltpu.CompilerParams(
            collective_id=0, has_side_effects=True, vmem_limit_bytes=54976 * 1024),
    )(slab_panel.reshape(SIDE, SIDE), slab_pattern, inner_panel.reshape(BW, SIDE), inner_pattern,
      slab_rows, column_ids)


def solution(mesh):
    return jax.shard_map(
        on_device,
        mesh=mesh,
        in_specs=(
            P("row", "layer", "col"),
            P("row", "layer", "col"),
            P("layer", "row", "col"),
            P("layer", "row", "col"),
            P("row"),
            P("col"),
        ),
        out_specs=P("row", ("col", "layer")),
        check_vma=False,
    )
```

```python
import jax
import jax.numpy as jnp
from jax import lax
from jax.experimental import pallas as pl
from jax.experimental.pallas import tpu as pltpu
from jax.sharding import PartitionSpec as P

MESH = pl.DeviceIdType.MESH
BW = 256
NY, NZ, NX = 8, 8, 4
SIDE = 512
PIECES = (128, 128, 128, 128)
STARTS = tuple(sum(PIECES[:q]) for q in range(len(PIECES)))
Q = len(PIECES)
PB = 2
BP = BW // PB

OTHER_PLANES = (
    ("first_slab", 2), ("send_slab", 3), ("send_slab", 0), ("send_slab", 1), ("send_inner",),
    ("share_inner",), ("slab", 2, 1), ("inner", 0, 1), ("inner", 1, 1), ("slab", 0, 1), ("slab", 3, 1),
    ("inner", 0, 2), ("inner", 1, 2), ("slab", 2, 2), ("slab", 1, 1), ("inner", 0, 3), ("slab", 0, 2),
    ("inner", 1, 3), ("inner", 0, 4), ("inner", 1, 4), ("slab", 2, 3), ("wait_core",), ("multiply", 0, 4, 0),
    ("multiply", 0, 4, 1), ("multiply", 0, 1, 2), ("multiply", 2, 1, 2), ("multiply", 2, 1, 3),
    ("slab", 1, 2), ("multiply", 1, 1, 2), ("slab", 0, 3), ("multiply", 0, 1, 3), ("slab", 3, 2),
    ("multiply", 3, 1, 2), ("slab", 2, 4), ("multiply", 2, 1, 4), ("meet", "x"), ("parts", 2), ("slab", 1, 3),
    ("multiply", 1, 1, 3), ("slab", 0, 4), ("multiply", 0, 1, 4), ("parts", 0), ("slab", 3, 3),
    ("multiply", 3, 1, 3), ("slab", 1, 4), ("multiply", 1, 1, 4), ("parts", 1), ("slab", 3, 4),
    ("multiply", 3, 1, 4), ("parts", 3), ("finish", 2), ("finish", 0), ("finish", 1), ("end",), ("finish", 3),
)
NEAR_PLANES = (
    ("first_slab", 2), ("send_slab", 3), ("send_slab", 0), ("send_slab", 1), ("send_inner",),
    ("share_inner",), ("slab", 2, 1), ("inner", 0, 1), ("slab", 0, 1), ("slab", 3, 1), ("inner", 1, 1),
    ("inner", 0, 2), ("slab", 2, 2), ("slab", 1, 1), ("inner", 1, 2), ("slab", 0, 2), ("inner", 0, 3),
    ("inner", 1, 3), ("slab", 2, 3), ("inner", 0, 4), ("inner", 1, 4), ("slab", 1, 2), ("wait_core",),
    ("multiply", 0, 4, 0), ("multiply", 0, 4, 1), ("multiply", 0, 3, 2), ("multiply", 2, 1, 3),
    ("slab", 0, 3), ("multiply", 0, 1, 3), ("slab", 3, 2), ("multiply", 3, 1, 2), ("slab", 2, 4),
    ("multiply", 2, 1, 4), ("meet", "x"), ("parts", 2), ("slab", 1, 3), ("multiply", 1, 1, 3), ("slab", 0, 4),
    ("multiply", 0, 1, 4), ("parts", 0), ("slab", 3, 3), ("multiply", 3, 1, 3), ("slab", 1, 4),
    ("multiply", 1, 1, 4), ("parts", 1), ("slab", 3, 4), ("multiply", 3, 1, 4), ("parts", 3), ("finish", 2),
    ("finish", 0), ("finish", 1), ("end",), ("finish", 3),
)
FIRST_PLANE = (
    ("first_slab", 2), ("send_slab", 3), ("send_slab", 0), ("send_slab", 1), ("send_inner",),
    ("share_inner",), ("slab", 2, 1), ("slab", 0, 1), ("slab", 3, 1), ("inner", 0, 1), ("inner", 1, 1),
    ("slab", 2, 2), ("slab", 1, 1), ("inner", 0, 2), ("slab", 0, 2), ("inner", 1, 2), ("inner", 0, 3),
    ("slab", 2, 3), ("inner", 1, 3), ("slab", 1, 2), ("inner", 0, 4), ("inner", 1, 4), ("slab", 0, 3),
    ("slab", 3, 2), ("wait_core",), ("multiply", 0, 4, 0), ("multiply", 0, 4, 1), ("multiply", 0, 4, 2),
    ("multiply", 0, 1, 3), ("multiply", 2, 1, 3), ("slab", 2, 4), ("multiply", 2, 1, 4), ("meet", "x"),
    ("parts", 2), ("slab", 1, 3), ("multiply", 1, 1, 3), ("slab", 0, 4), ("multiply", 0, 1, 4), ("parts", 0),
    ("slab", 3, 3), ("multiply", 3, 1, 3), ("slab", 1, 4), ("multiply", 1, 1, 4), ("parts", 1),
    ("slab", 3, 4), ("multiply", 3, 1, 4), ("parts", 3), ("finish", 2), ("finish", 0), ("finish", 1),
    ("end",), ("finish", 3),
)


def kernel(slab, slab_pat, inner, inner_pat, row_ids, col_ids, out,
           a_raw, b_raw, a_all, b_all, acc, rs,
           meet_sem, ld_sem, as_sem, ar_sem, bs_sem, br_sem, ss_sem, sr_sem, cs_sem, cr_sem):
    r, y, x = lax.axis_index("row"), lax.axis_index("col"), lax.axis_index("layer")
    z, c = r // 2, r % 2
    y_to = [(r, (y + 1) % NY, x), (r, (y + NY - 1) % NY, x)]
    z_to = [(((z + 1) % NZ) * 2 + c, y, x), (((z + NZ - 1) % NZ) * 2 + c, y, x)]
    sibling = (z * 2 + 1 - c, y, x)
    x_to = [(r, y, (x + d) % NX) for d in range(1, NX)]
    gray = (0, 1, 3, 2)

    def before(a, b, order):
        less = [jnp.logical_and(a == i, b == k) for i in range(len(order)) for k in range(len(order))
                if order[i] < order[k]]
        out = less[0]
        for term in less[1:]:
            out = jnp.logical_or(out, term)
        return out

    z_rank = gray + tuple(range(4, NZ))
    pairs = {
        "core": [(sibling, c == 0)],
        "x": [(peer, before(x, (x + d) % NX, gray)) for d, peer in enumerate(x_to, 1)],
        "up": [(z_to[0], before(z, (z + 1) % NZ, z_rank))],
        "down": [(z_to[1], before(z, (z + NZ - 1) % NZ, z_rank))],
    }
    answer = {"core": meet_sem.at[0], "x": meet_sem.at[1], "up": meet_sem.at[3], "down": meet_sem.at[2]}
    mine = {"core": meet_sem.at[0], "x": meet_sem.at[1], "up": meet_sem.at[2], "down": meet_sem.at[3]}

    def signal(sem, peer):
        pl.semaphore_signal(sem, inc=1, device_id=peer, device_id_type=MESH)

    barrier = pltpu.get_barrier_semaphore()
    for peer in y_to:
        signal(barrier, peer)
    for kind in pairs:
        for peer, first in pairs[kind]:
            pl.when(first)(lambda peer=peer: signal(barrier, peer))

    def count(flags):
        return sum(jnp.where(flag, 1, 0) for flag in flags)

    def enter():
        seconds = [jnp.logical_not(first) for kind in pairs for _, first in pairs[kind]]
        pl.semaphore_wait(barrier, len(y_to) + count(seconds))

    def reply():
        for kind in pairs:
            for peer, first in pairs[kind]:
                pl.when(jnp.logical_not(first))(lambda kind=kind, peer=peer: signal(answer[kind], peer))

    def meet(kind):
        firsts = count([first for _, first in pairs[kind]])
        pl.when(firsts > 0)(lambda: pl.semaphore_wait(mine[kind], firsts))

    def spans(q):
        for i in range(SIDE // BW):
            lo, hi = max(STARTS[q], i * BW), min(STARTS[q] + PIECES[q], (i + 1) * BW)
            if lo < hi:
                yield i, lo, hi - lo

    loads = [
        pltpu.make_async_copy(slab.at[pl.ds(STARTS[q], n)], a_raw.at[pl.ds(STARTS[q], n)], ld_sem.at[q])
        for q, n in enumerate(PIECES)
    ] + [pltpu.make_async_copy(inner, b_raw, ld_sem.at[Q])]
    for i in [0, Q] + list(range(1, Q)):
        loads[i].start()

    def mask_slab(q):
        loads[q].wait()
        for i, lo, n in spans(q):
            for j in range(SIDE // BW):
                keep = slab_pat[i, 0, j].astype(jnp.float32).astype(jnp.bfloat16)
                at = (pl.ds(lo, n), pl.ds(j * BW, BW))
                a_all[(y, *at)] = a_raw[at] * keep

    def mask_inner():
        loads[Q].wait()
        for j in range(SIDE // BW):
            keep = inner_pat[0, 0, j].astype(jnp.float32).astype(jnp.bfloat16)
            cols = pl.ds(j * BW, BW)
            b_all[z, pl.ds(c * BW, BW), cols] = b_raw[:, cols] * keep

    def source(me, size, way, d):
        return (me + size - d) % size if way == 0 else (me + d) % size

    sends = []

    def start(copy):
        copy.start()
        sends.append(copy)

    def slab_copy(way, q, d, hop):
        n = PIECES[q] if hop < 3 else PIECES[q] // 2
        lo = STARTS[q] + (way * n if hop == 3 else 0)
        ref = a_all.at[source(y, NY, way, d), pl.ds(lo, n)]
        return pltpu.make_async_remote_copy(
            src_ref=ref, dst_ref=ref, send_sem=as_sem.at[way, q, hop], recv_sem=ar_sem.at[way, q, hop],
            device_id=y_to[way], device_id_type=MESH)

    def inner_ref(p, way, d, core, half):
        n = BP // 2 if half else BP
        lo = core * BW + p * BP + (way * n if half else 0)
        return b_all.at[source(z, NZ, way, d), pl.ds(lo, n)]

    def inner_copy(p, way, d, hop):
        ref = inner_ref(p, way, d, c, hop == 3)
        return pltpu.make_async_remote_copy(
            src_ref=ref, dst_ref=ref, send_sem=bs_sem.at[p, way, hop], recv_sem=br_sem.at[p, way, hop],
            device_id=z_to[way], device_id_type=MESH)

    def core_copy(p, way, d, core):
        ref = inner_ref(p, way, d, core, d == 4)
        return pltpu.make_async_remote_copy(
            src_ref=ref, dst_ref=ref, send_sem=ss_sem.at[p, way, d], recv_sem=sr_sem.at[p, way, d],
            device_id=sibling, device_id_type=MESH)

    def part_copy(q, d):
        rows = pl.ds(STARTS[q], PIECES[q])
        return pltpu.make_async_remote_copy(
            src_ref=acc.at[(x + d) % NX, rows], dst_ref=rs.at[d - 1, rows],
            send_sem=cs_sem.at[q, d - 1], recv_sem=cr_sem.at[q, d - 1],
            device_id=x_to[d - 1], device_id_type=MESH)

    def send_slab(q):
        mask_slab(q)
        for way in range(2):
            start(slab_copy(way, q, 0, 0))

    def send_inner():
        mask_inner()
        for way, kind in enumerate(("up", "down")):
            meet(kind)
            for p in range(PB):
                start(inner_copy(p, way, 0, 0))

    def share_inner():
        meet("core")
        for p in range(PB):
            start(core_copy(p, 0, 0, c))

    def pass_slab(q, d):
        for way in range(2):
            slab_copy(way, q, d, d - 1).wait_recv()
            if d < 4:
                start(slab_copy(way, q, d, d))

    def pass_inner(p, d):
        for way in range(2):
            inner_copy(p, way, d, d - 1).wait_recv()
            if d < 4:
                start(inner_copy(p, way, d, d))
            start(core_copy(p, way, d, c))

    def wait_core():
        for d in range(5):
            for way in range(2 if d else 1):
                for p in range(PB):
                    core_copy(p, way, d, 1 - c).wait_recv()

    def multiply(q0, nq, d):
        rows = pl.ds(STARTS[q0], sum(PIECES[q0:q0 + nq]))
        for way in range(2 if 0 < d < 4 else 1):
            src = source(y, NY, way, d)
            product = jnp.dot(a_all[src, rows, :], b_all[src], preferred_element_type=jnp.float32)
            for k in range(NX):
                part = product[:, k * 128:(k + 1) * 128]
                acc[k, rows] = part if d == 0 else acc[k, rows] + part

    def send_parts(q):
        for d in (2, 1, 3):
            start(part_copy(q, d))

    def finish(q):
        for d in range(1, NX):
            part_copy(q, d).wait_recv()
        for i, lo, n in spans(q):
            rows = pl.ds(lo, n)
            total = acc[x, rows] + rs[0, rows] + rs[1, rows] + rs[2, rows]
            keep = col_ids[x // 2] >= row_ids[i]
            out[rows, :] = jnp.where(keep, total, 0.0).astype(jnp.bfloat16)

    def end():
        for copy in sends:
            copy.wait_send()

    def first_slab(q):
        mask_slab(q)
        enter()
        for way in range(2):
            start(slab_copy(way, q, 0, 0))
        reply()

    steps = {
        "first_slab": first_slab, "meet": meet, "send_slab": send_slab, "send_inner": send_inner,
        "share_inner": share_inner, "slab": pass_slab, "inner": pass_inner,
        "wait_core": wait_core, "multiply": multiply, "parts": send_parts, "finish": finish, "end": end,
    }

    def run(schedule):
        sends.clear()
        for name, *args in schedule:
            steps[name](*args)

    pl.when(z == 0)(lambda: run(FIRST_PLANE))
    pl.when(jnp.logical_and(z > 0, z <= 2))(lambda: run(NEAR_PLANES))
    pl.when(z > 2)(lambda: run(OTHER_PLANES))


def on_device(slab_panel, slab_pattern, inner_panel, inner_pattern, slab_rows, column_ids):
    whole = pl.BlockSpec(memory_space=pl.ANY)
    scalars = pl.BlockSpec(memory_space=pltpu.SMEM)
    dma = pltpu.SemaphoreType.DMA
    return pl.pallas_call(
        kernel,
        out_shape=jax.ShapeDtypeStruct((SIDE, 128), jnp.bfloat16),
        in_specs=[whole, scalars, whole, scalars, scalars, scalars],
        out_specs=pl.BlockSpec(memory_space=pltpu.VMEM),
        scratch_shapes=[
            pltpu.VMEM((SIDE, SIDE), jnp.bfloat16),
            pltpu.VMEM((BW, SIDE), jnp.bfloat16),
            pltpu.VMEM((NY, SIDE, SIDE), jnp.bfloat16),
            pltpu.VMEM((NZ, SIDE, SIDE), jnp.bfloat16),
            pltpu.VMEM((NX, SIDE, 128), jnp.float32),
            pltpu.VMEM((NX - 1, SIDE, 128), jnp.float32),
            pltpu.SemaphoreType.REGULAR((4,)),
            dma((Q + 1,)),
            dma((2, Q, 4)), dma((2, Q, 4)),
            dma((PB, 2, 4)), dma((PB, 2, 4)),
            dma((PB, 2, 5)), dma((PB, 2, 5)),
            dma((Q, NX - 1)), dma((Q, NX - 1)),
        ],
        compiler_params=pltpu.CompilerParams(
            collective_id=0, has_side_effects=True, vmem_limit_bytes=54976 * 1024),
    )(slab_panel.reshape(SIDE, SIDE), slab_pattern, inner_panel.reshape(BW, SIDE), inner_pattern,
      slab_rows, column_ids)


def solution(mesh):
    return jax.shard_map(
        on_device,
        mesh=mesh,
        in_specs=(
            P("row", "layer", "col"),
            P("row", "layer", "col"),
            P("layer", "row", "col"),
            P("layer", "row", "col"),
            P("row"),
            P("col"),
        ),
        out_specs=P("row", ("col", "layer")),
        check_vma=False,
    )
```

```python
import jax
import jax.numpy as jnp
from jax import lax
from jax.experimental import pallas as pl
from jax.experimental.pallas import tpu as pltpu
from jax.sharding import PartitionSpec as P

MESH = pl.DeviceIdType.MESH
BW = 256
NY, NZ, NX = 8, 8, 4
SIDE = 512
PIECES = (128, 128, 128, 128)
STARTS = tuple(sum(PIECES[:q]) for q in range(len(PIECES)))
Q = len(PIECES)
PB = 2
BP = BW // PB

FIRST_SLAB, SEND_SLAB, SEND_INNER, SHARE_INNER, SLAB, INNER, \
    WAIT_CORE, MULTIPLY, MEET, PARTS, FINISH, END = range(12)
CORE, X, UP, DOWN = range(4)
OTHER_PLANES = (
    (FIRST_SLAB, 2), (SEND_SLAB, 3), (SEND_SLAB, 0), (SEND_SLAB, 1), (SEND_INNER,),
    (SHARE_INNER,), (SLAB, 2, 1), (INNER, 0, 1), (INNER, 1, 1), (SLAB, 0, 1), (SLAB, 3, 1),
    (INNER, 0, 2), (INNER, 1, 2), (SLAB, 2, 2), (SLAB, 1, 1), (INNER, 0, 3), (SLAB, 0, 2),
    (INNER, 1, 3), (INNER, 0, 4), (INNER, 1, 4), (SLAB, 2, 3), (WAIT_CORE,), (MULTIPLY, 0, 4, 0),
    (MULTIPLY, 0, 4, 1), (MULTIPLY, 0, 1, 2), (MULTIPLY, 2, 1, 2), (MULTIPLY, 2, 1, 3),
    (SLAB, 1, 2), (MULTIPLY, 1, 1, 2), (SLAB, 0, 3), (MULTIPLY, 0, 1, 3), (SLAB, 3, 2),
    (MULTIPLY, 3, 1, 2), (SLAB, 2, 4), (MULTIPLY, 2, 1, 4), (MEET, X), (PARTS, 2), (SLAB, 1, 3),
    (MULTIPLY, 1, 1, 3), (SLAB, 0, 4), (MULTIPLY, 0, 1, 4), (PARTS, 0), (SLAB, 3, 3),
    (MULTIPLY, 3, 1, 3), (SLAB, 1, 4), (MULTIPLY, 1, 1, 4), (PARTS, 1), (SLAB, 3, 4),
    (MULTIPLY, 3, 1, 4), (PARTS, 3), (FINISH, 2), (FINISH, 0), (FINISH, 1), (END,), (FINISH, 3),
)
NEAR_PLANES = (
    (FIRST_SLAB, 2), (SEND_SLAB, 3), (SEND_SLAB, 0), (SEND_SLAB, 1), (SEND_INNER,),
    (SHARE_INNER,), (SLAB, 2, 1), (INNER, 0, 1), (SLAB, 0, 1), (SLAB, 3, 1), (INNER, 1, 1),
    (INNER, 0, 2), (SLAB, 2, 2), (SLAB, 1, 1), (INNER, 1, 2), (SLAB, 0, 2), (INNER, 0, 3),
    (INNER, 1, 3), (SLAB, 2, 3), (INNER, 0, 4), (INNER, 1, 4), (SLAB, 1, 2), (WAIT_CORE,),
    (MULTIPLY, 0, 4, 0), (MULTIPLY, 0, 4, 1), (MULTIPLY, 0, 3, 2), (MULTIPLY, 2, 1, 3),
    (SLAB, 0, 3), (MULTIPLY, 0, 1, 3), (SLAB, 3, 2), (MULTIPLY, 3, 1, 2), (SLAB, 2, 4),
    (MULTIPLY, 2, 1, 4), (MEET, X), (PARTS, 2), (SLAB, 1, 3), (MULTIPLY, 1, 1, 3), (SLAB, 0, 4),
    (MULTIPLY, 0, 1, 4), (PARTS, 0), (SLAB, 3, 3), (MULTIPLY, 3, 1, 3), (SLAB, 1, 4),
    (MULTIPLY, 1, 1, 4), (PARTS, 1), (SLAB, 3, 4), (MULTIPLY, 3, 1, 4), (PARTS, 3), (FINISH, 2),
    (FINISH, 0), (FINISH, 1), (END,), (FINISH, 3),
)
FIRST_PLANE = (
    (FIRST_SLAB, 2), (SEND_SLAB, 3), (SEND_SLAB, 0), (SEND_SLAB, 1), (SEND_INNER,),
    (SHARE_INNER,), (SLAB, 2, 1), (SLAB, 0, 1), (SLAB, 3, 1), (INNER, 0, 1), (INNER, 1, 1),
    (SLAB, 2, 2), (SLAB, 1, 1), (INNER, 0, 2), (SLAB, 0, 2), (INNER, 1, 2), (INNER, 0, 3),
    (SLAB, 2, 3), (INNER, 1, 3), (SLAB, 1, 2), (INNER, 0, 4), (INNER, 1, 4), (SLAB, 0, 3),
    (SLAB, 3, 2), (WAIT_CORE,), (MULTIPLY, 0, 4, 0), (MULTIPLY, 0, 4, 1), (MULTIPLY, 0, 4, 2),
    (MULTIPLY, 0, 1, 3), (MULTIPLY, 2, 1, 3), (SLAB, 2, 4), (MULTIPLY, 2, 1, 4), (MEET, X),
    (PARTS, 2), (SLAB, 1, 3), (MULTIPLY, 1, 1, 3), (SLAB, 0, 4), (MULTIPLY, 0, 1, 4), (PARTS, 0),
    (SLAB, 3, 3), (MULTIPLY, 3, 1, 3), (SLAB, 1, 4), (MULTIPLY, 1, 1, 4), (PARTS, 1),
    (SLAB, 3, 4), (MULTIPLY, 3, 1, 4), (PARTS, 3), (FINISH, 2), (FINISH, 0), (FINISH, 1),
    (END,), (FINISH, 3),
)


def kernel(slab, slab_pat, inner, inner_pat, row_ids, col_ids, out,
           a_raw, b_raw, a_all, b_all, acc, rs,
           meet_sem, ld_sem, as_sem, ar_sem, bs_sem, br_sem, ss_sem, sr_sem, cs_sem, cr_sem):
    r, y, x = lax.axis_index("row"), lax.axis_index("col"), lax.axis_index("layer")
    z, c = r // 2, r % 2
    y_to = [(r, (y + 1) % NY, x), (r, (y + NY - 1) % NY, x)]
    z_to = [(((z + 1) % NZ) * 2 + c, y, x), (((z + NZ - 1) % NZ) * 2 + c, y, x)]
    sibling = (z * 2 + 1 - c, y, x)
    x_to = [(r, y, (x + d) % NX) for d in range(1, NX)]
    gray = (0, 1, 3, 2)

    def before(a, b, order):
        less = [jnp.logical_and(a == i, b == k) for i in range(len(order)) for k in range(len(order))
                if order[i] < order[k]]
        out = less[0]
        for term in less[1:]:
            out = jnp.logical_or(out, term)
        return out

    z_rank = gray + tuple(range(4, NZ))
    pairs = {
        CORE: [(sibling, c == 0)],
        X: [(peer, before(x, (x + d) % NX, gray)) for d, peer in enumerate(x_to, 1)],
        UP: [(z_to[0], before(z, (z + 1) % NZ, z_rank))],
        DOWN: [(z_to[1], before(z, (z + NZ - 1) % NZ, z_rank))],
    }
    answer = {CORE: meet_sem.at[0], X: meet_sem.at[1], UP: meet_sem.at[3], DOWN: meet_sem.at[2]}
    mine = {CORE: meet_sem.at[0], X: meet_sem.at[1], UP: meet_sem.at[2], DOWN: meet_sem.at[3]}

    def signal(sem, peer):
        pl.semaphore_signal(sem, inc=1, device_id=peer, device_id_type=MESH)

    barrier = pltpu.get_barrier_semaphore()
    for peer in y_to:
        signal(barrier, peer)
    for kind in pairs:
        for peer, first in pairs[kind]:
            pl.when(first)(lambda peer=peer: signal(barrier, peer))

    def count(flags):
        return sum(jnp.where(flag, 1, 0) for flag in flags)

    def enter():
        seconds = [jnp.logical_not(first) for kind in pairs for _, first in pairs[kind]]
        pl.semaphore_wait(barrier, len(y_to) + count(seconds))

    def reply():
        for kind in pairs:
            for peer, first in pairs[kind]:
                pl.when(jnp.logical_not(first))(lambda kind=kind, peer=peer: signal(answer[kind], peer))

    def meet(kind):
        firsts = count([first for _, first in pairs[kind]])
        pl.when(firsts > 0)(lambda: pl.semaphore_wait(mine[kind], firsts))

    def spans(q):
        for i in range(SIDE // BW):
            lo, hi = max(STARTS[q], i * BW), min(STARTS[q] + PIECES[q], (i + 1) * BW)
            if lo < hi:
                yield i, lo, hi - lo

    loads = [
        pltpu.make_async_copy(slab.at[pl.ds(STARTS[q], n)], a_raw.at[pl.ds(STARTS[q], n)], ld_sem.at[q])
        for q, n in enumerate(PIECES)
    ] + [pltpu.make_async_copy(inner, b_raw, ld_sem.at[Q])]
    for i in [0, Q] + list(range(1, Q)):
        loads[i].start()

    def mask_slab(q):
        loads[q].wait()
        for i, lo, n in spans(q):
            for j in range(SIDE // BW):
                keep = slab_pat[i, 0, j].astype(jnp.float32).astype(jnp.bfloat16)
                at = (pl.ds(lo, n), pl.ds(j * BW, BW))
                a_all[(y, *at)] = a_raw[at] * keep

    def mask_inner():
        loads[Q].wait()
        for j in range(SIDE // BW):
            keep = inner_pat[0, 0, j].astype(jnp.float32).astype(jnp.bfloat16)
            cols = pl.ds(j * BW, BW)
            b_all[z, pl.ds(c * BW, BW), cols] = b_raw[:, cols] * keep

    def source(me, size, way, d):
        return (me + size - d) % size if way == 0 else (me + d) % size

    sends = []

    def start(copy):
        copy.start()
        sends.append(copy)

    def slab_copy(way, q, d, hop):
        n = PIECES[q] if hop < 3 else PIECES[q] // 2
        lo = STARTS[q] + (way * n if hop == 3 else 0)
        ref = a_all.at[source(y, NY, way, d), pl.ds(lo, n)]
        return pltpu.make_async_remote_copy(
            src_ref=ref, dst_ref=ref, send_sem=as_sem.at[way, q, hop], recv_sem=ar_sem.at[way, q, hop],
            device_id=y_to[way], device_id_type=MESH)

    def inner_ref(p, way, d, core, half):
        n = BP // 2 if half else BP
        lo = core * BW + p * BP + (way * n if half else 0)
        return b_all.at[source(z, NZ, way, d), pl.ds(lo, n)]

    def inner_copy(p, way, d, hop):
        ref = inner_ref(p, way, d, c, hop == 3)
        return pltpu.make_async_remote_copy(
            src_ref=ref, dst_ref=ref, send_sem=bs_sem.at[p, way, hop], recv_sem=br_sem.at[p, way, hop],
            device_id=z_to[way], device_id_type=MESH)

    def core_copy(p, way, d, core):
        ref = inner_ref(p, way, d, core, d == 4)
        return pltpu.make_async_remote_copy(
            src_ref=ref, dst_ref=ref, send_sem=ss_sem.at[p, way, d], recv_sem=sr_sem.at[p, way, d],
            device_id=sibling, device_id_type=MESH)

    def part_copy(q, d):
        rows = pl.ds(STARTS[q], PIECES[q])
        return pltpu.make_async_remote_copy(
            src_ref=acc.at[(x + d) % NX, rows], dst_ref=rs.at[d - 1, rows],
            send_sem=cs_sem.at[q, d - 1], recv_sem=cr_sem.at[q, d - 1],
            device_id=x_to[d - 1], device_id_type=MESH)

    def send_slab(q):
        mask_slab(q)
        for way in range(2):
            start(slab_copy(way, q, 0, 0))

    def send_inner():
        mask_inner()
        for way, kind in enumerate((UP, DOWN)):
            meet(kind)
            for p in range(PB):
                start(inner_copy(p, way, 0, 0))

    def share_inner():
        meet(CORE)
        for p in range(PB):
            start(core_copy(p, 0, 0, c))

    def pass_slab(q, d):
        for way in range(2):
            slab_copy(way, q, d, d - 1).wait_recv()
            if d < 4:
                start(slab_copy(way, q, d, d))

    def pass_inner(p, d):
        for way in range(2):
            inner_copy(p, way, d, d - 1).wait_recv()
            if d < 4:
                start(inner_copy(p, way, d, d))
            start(core_copy(p, way, d, c))

    def wait_core():
        for d in range(5):
            for way in range(2 if d else 1):
                for p in range(PB):
                    core_copy(p, way, d, 1 - c).wait_recv()

    def multiply(q0, nq, d):
        rows = pl.ds(STARTS[q0], sum(PIECES[q0:q0 + nq]))
        for way in range(2 if 0 < d < 4 else 1):
            src = source(y, NY, way, d)
            product = jnp.dot(a_all[src, rows, :], b_all[src], preferred_element_type=jnp.float32)
            for k in range(NX):
                part = product[:, k * 128:(k + 1) * 128]
                acc[k, rows] = part if d == 0 else acc[k, rows] + part

    def send_parts(q):
        for d in (2, 1, 3):
            start(part_copy(q, d))

    def finish(q):
        for d in range(1, NX):
            part_copy(q, d).wait_recv()
        for i, lo, n in spans(q):
            rows = pl.ds(lo, n)
            total = acc[x, rows] + rs[0, rows] + rs[1, rows] + rs[2, rows]
            keep = col_ids[x // 2] >= row_ids[i]
            out[rows, :] = jnp.where(keep, total, 0.0).astype(jnp.bfloat16)

    def end():
        for copy in sends:
            copy.wait_send()

    def first_slab(q):
        mask_slab(q)
        enter()
        for way in range(2):
            start(slab_copy(way, q, 0, 0))
        reply()

    steps = {
        FIRST_SLAB: first_slab, SEND_SLAB: send_slab, SEND_INNER: send_inner, SHARE_INNER: share_inner,
        SLAB: pass_slab, INNER: pass_inner, WAIT_CORE: wait_core, MULTIPLY: multiply, MEET: meet,
        PARTS: send_parts, FINISH: finish, END: end,
    }

    def run(schedule):
        sends.clear()
        for name, *args in schedule:
            steps[name](*args)

    pl.when(z == 0)(lambda: run(FIRST_PLANE))
    pl.when(jnp.logical_and(z > 0, z <= 2))(lambda: run(NEAR_PLANES))
    pl.when(z > 2)(lambda: run(OTHER_PLANES))


def on_device(slab_panel, slab_pattern, inner_panel, inner_pattern, slab_rows, column_ids):
    whole = pl.BlockSpec(memory_space=pl.ANY)
    scalars = pl.BlockSpec(memory_space=pltpu.SMEM)
    dma = pltpu.SemaphoreType.DMA
    return pl.pallas_call(
        kernel,
        out_shape=jax.ShapeDtypeStruct((SIDE, 128), jnp.bfloat16),
        in_specs=[whole, scalars, whole, scalars, scalars, scalars],
        out_specs=pl.BlockSpec(memory_space=pltpu.VMEM),
        scratch_shapes=[
            pltpu.VMEM((SIDE, SIDE), jnp.bfloat16),
            pltpu.VMEM((BW, SIDE), jnp.bfloat16),
            pltpu.VMEM((NY, SIDE, SIDE), jnp.bfloat16),
            pltpu.VMEM((NZ, SIDE, SIDE), jnp.bfloat16),
            pltpu.VMEM((NX, SIDE, 128), jnp.float32),
            pltpu.VMEM((NX - 1, SIDE, 128), jnp.float32),
            pltpu.SemaphoreType.REGULAR((4,)),
            dma((Q + 1,)),
            dma((2, Q, 4)), dma((2, Q, 4)),
            dma((PB, 2, 4)), dma((PB, 2, 4)),
            dma((PB, 2, 5)), dma((PB, 2, 5)),
            dma((Q, NX - 1)), dma((Q, NX - 1)),
        ],
        compiler_params=pltpu.CompilerParams(
            collective_id=0, has_side_effects=True, vmem_limit_bytes=54976 * 1024),
    )(slab_panel.reshape(SIDE, SIDE), slab_pattern, inner_panel.reshape(BW, SIDE), inner_pattern,
      slab_rows, column_ids)


def solution(mesh):
    return jax.shard_map(
        on_device,
        mesh=mesh,
        in_specs=(
            P("row", "layer", "col"),
            P("row", "layer", "col"),
            P("layer", "row", "col"),
            P("layer", "row", "col"),
            P("row"),
            P("col"),
        ),
        out_specs=P("row", ("col", "layer")),
        check_vma=False,
    )
```

```python
import jax
import jax.numpy as jnp
from jax import lax
from jax.experimental import pallas as pl
from jax.experimental.pallas import tpu as pltpu
from jax.sharding import PartitionSpec as P

MESH = pl.DeviceIdType.MESH
BW = 256
NY, NZ, NX = 8, 8, 4
SIDE = 512
PIECES = (128, 128, 128, 128)
STARTS = tuple(sum(PIECES[:q]) for q in range(len(PIECES)))
Q = len(PIECES)
PB = 2
BP = BW // PB

FIRST_SLAB, SEND_SLAB, SEND_INNER, SHARE_INNER, SLAB, INNER, \
    WAIT_CORE, MULTIPLY, MEET, PARTS, FINISH, END = range(12)
CORE, X, UP, DOWN = range(4)
OTHER_PLANES = (
    (FIRST_SLAB, 2), (SEND_SLAB, 3), (SEND_SLAB, 0), (SEND_SLAB, 1), (SEND_INNER,),
    (SHARE_INNER,), (SLAB, 2, 1), (INNER, 0, 1), (INNER, 1, 1), (SLAB, 0, 1), (SLAB, 3, 1),
    (INNER, 0, 2), (INNER, 1, 2), (SLAB, 2, 2), (SLAB, 1, 1), (INNER, 0, 3), (SLAB, 0, 2),
    (INNER, 1, 3), (INNER, 0, 4), (INNER, 1, 4), (SLAB, 2, 3), (WAIT_CORE,), (MULTIPLY, 0, 4, 0),
    (MULTIPLY, 0, 4, 1), (MULTIPLY, 0, 1, 2), (MULTIPLY, 2, 1, 2), (MULTIPLY, 2, 1, 3),
    (SLAB, 1, 2), (MULTIPLY, 1, 1, 2), (SLAB, 0, 3), (MULTIPLY, 0, 1, 3), (SLAB, 3, 2),
    (MULTIPLY, 3, 1, 2), (SLAB, 2, 4), (MULTIPLY, 2, 1, 4), (MEET, X), (PARTS, 2), (SLAB, 1, 3),
    (MULTIPLY, 1, 1, 3), (SLAB, 0, 4), (MULTIPLY, 0, 1, 4), (PARTS, 0), (SLAB, 3, 3),
    (MULTIPLY, 3, 1, 3), (SLAB, 1, 4), (MULTIPLY, 1, 1, 4), (PARTS, 1), (FINISH, 2), (SLAB, 3, 4),
    (MULTIPLY, 3, 1, 4), (PARTS, 3),  (FINISH, 0), (FINISH, 1), (END,), (FINISH, 3),
)
NEAR_PLANES = (
    (FIRST_SLAB, 2), (SEND_SLAB, 3), (SEND_SLAB, 0), (SEND_SLAB, 1), (SEND_INNER,),
    (SHARE_INNER,), (SLAB, 2, 1), (INNER, 0, 1), (SLAB, 0, 1), (SLAB, 3, 1), (INNER, 1, 1),
    (INNER, 0, 2), (SLAB, 2, 2), (SLAB, 1, 1), (INNER, 1, 2), (SLAB, 0, 2), (INNER, 0, 3),
    (INNER, 1, 3), (SLAB, 2, 3), (INNER, 0, 4), (INNER, 1, 4), (SLAB, 1, 2), (WAIT_CORE,),
    (MULTIPLY, 0, 4, 0), (MULTIPLY, 0, 4, 1), (MULTIPLY, 0, 3, 2), (MULTIPLY, 2, 1, 3),
    (SLAB, 0, 3), (MULTIPLY, 0, 1, 3), (SLAB, 3, 2), (MULTIPLY, 3, 1, 2), (SLAB, 2, 4),
    (MULTIPLY, 2, 1, 4), (MEET, X), (PARTS, 2), (SLAB, 1, 3), (MULTIPLY, 1, 1, 3), (SLAB, 0, 4),
    (MULTIPLY, 0, 1, 4), (PARTS, 0), (SLAB, 3, 3), (MULTIPLY, 3, 1, 3), (SLAB, 1, 4),
    (MULTIPLY, 1, 1, 4), (PARTS, 1), (FINISH, 2), (SLAB, 3, 4), (MULTIPLY, 3, 1, 4), (PARTS, 3),
    (FINISH, 0), (FINISH, 1), (END,), (FINISH, 3),
)
FIRST_PLANE = (
    (FIRST_SLAB, 2), (SEND_SLAB, 3), (SEND_SLAB, 0), (SEND_SLAB, 1), (SEND_INNER,),
    (SHARE_INNER,), (SLAB, 2, 1), (SLAB, 0, 1), (SLAB, 3, 1), (INNER, 0, 1), (INNER, 1, 1),
    (SLAB, 2, 2), (SLAB, 1, 1), (INNER, 0, 2), (SLAB, 0, 2), (INNER, 1, 2), (INNER, 0, 3),
    (SLAB, 2, 3), (INNER, 1, 3), (SLAB, 1, 2), (INNER, 0, 4), (INNER, 1, 4), (SLAB, 0, 3),
    (SLAB, 3, 2), (WAIT_CORE,), (MULTIPLY, 0, 4, 0), (MULTIPLY, 0, 4, 1), (MULTIPLY, 0, 4, 2),
    (MULTIPLY, 0, 1, 3), (MULTIPLY, 2, 1, 3), (SLAB, 2, 4), (MULTIPLY, 2, 1, 4), (MEET, X),
    (PARTS, 2), (SLAB, 1, 3), (MULTIPLY, 1, 1, 3), (SLAB, 0, 4), (MULTIPLY, 0, 1, 4), (PARTS, 0),
    (SLAB, 3, 3), (MULTIPLY, 3, 1, 3), (SLAB, 1, 4), (MULTIPLY, 1, 1, 4), (PARTS, 1), (FINISH, 2),
    (SLAB, 3, 4), (MULTIPLY, 3, 1, 4), (PARTS, 3),  (FINISH, 0), (FINISH, 1),
    (END,), (FINISH, 3),
)


def kernel(slab, slab_pat, inner, inner_pat, row_ids, col_ids, out,
           a_raw, b_raw, a_all, b_all, acc, rs,
           meet_sem, ld_sem, as_sem, ar_sem, bs_sem, br_sem, ss_sem, sr_sem, cs_sem, cr_sem):
    r, y, x = lax.axis_index("row"), lax.axis_index("col"), lax.axis_index("layer")
    z, c = r // 2, r % 2
    y_to = [(r, (y + 1) % NY, x), (r, (y + NY - 1) % NY, x)]
    z_to = [(((z + 1) % NZ) * 2 + c, y, x), (((z + NZ - 1) % NZ) * 2 + c, y, x)]
    sibling = (z * 2 + 1 - c, y, x)
    x_to = [(r, y, (x + d) % NX) for d in range(1, NX)]
    gray = (0, 1, 3, 2)

    def before(a, b, order):
        less = [jnp.logical_and(a == i, b == k) for i in range(len(order)) for k in range(len(order))
                if order[i] < order[k]]
        out = less[0]
        for term in less[1:]:
            out = jnp.logical_or(out, term)
        return out

    z_rank = gray + tuple(range(4, NZ))
    pairs = {
        CORE: [(sibling, c == 0)],
        X: [(peer, before(x, (x + d) % NX, gray)) for d, peer in enumerate(x_to, 1)],
        UP: [(z_to[0], before(z, (z + 1) % NZ, z_rank))],
        DOWN: [(z_to[1], before(z, (z + NZ - 1) % NZ, z_rank))],
    }
    answer = {CORE: meet_sem.at[0], X: meet_sem.at[1], UP: meet_sem.at[3], DOWN: meet_sem.at[2]}
    mine = {CORE: meet_sem.at[0], X: meet_sem.at[1], UP: meet_sem.at[2], DOWN: meet_sem.at[3]}

    def signal(sem, peer):
        pl.semaphore_signal(sem, inc=1, device_id=peer, device_id_type=MESH)

    barrier = pltpu.get_barrier_semaphore()
    for peer in y_to:
        signal(barrier, peer)
    for kind in pairs:
        for peer, first in pairs[kind]:
            pl.when(first)(lambda peer=peer: signal(barrier, peer))

    def count(flags):
        return sum(jnp.where(flag, 1, 0) for flag in flags)

    def enter():
        seconds = [jnp.logical_not(first) for kind in pairs for _, first in pairs[kind]]
        pl.semaphore_wait(barrier, len(y_to) + count(seconds))

    def reply():
        for kind in pairs:
            for peer, first in pairs[kind]:
                pl.when(jnp.logical_not(first))(lambda kind=kind, peer=peer: signal(answer[kind], peer))

    def meet(kind):
        firsts = count([first for _, first in pairs[kind]])
        pl.when(firsts > 0)(lambda: pl.semaphore_wait(mine[kind], firsts))

    def spans(q):
        for i in range(SIDE // BW):
            lo, hi = max(STARTS[q], i * BW), min(STARTS[q] + PIECES[q], (i + 1) * BW)
            if lo < hi:
                yield i, lo, hi - lo

    loads = [
        pltpu.make_async_copy(slab.at[pl.ds(STARTS[q], n)], a_raw.at[pl.ds(STARTS[q], n)], ld_sem.at[q])
        for q, n in enumerate(PIECES)
    ] + [pltpu.make_async_copy(inner, b_raw, ld_sem.at[Q])]
    for i in [0, Q] + list(range(1, Q)):
        loads[i].start()

    def mask_slab(q):
        loads[q].wait()
        for i, lo, n in spans(q):
            for j in range(SIDE // BW):
                keep = slab_pat[i, 0, j].astype(jnp.float32).astype(jnp.bfloat16)
                at = (pl.ds(lo, n), pl.ds(j * BW, BW))
                a_all[(y, *at)] = a_raw[at] * keep

    def mask_inner():
        loads[Q].wait()
        for j in range(SIDE // BW):
            keep = inner_pat[0, 0, j].astype(jnp.float32).astype(jnp.bfloat16)
            cols = pl.ds(j * BW, BW)
            b_all[z, pl.ds(c * BW, BW), cols] = b_raw[:, cols] * keep

    def source(me, size, way, d):
        return (me + size - d) % size if way == 0 else (me + d) % size

    sends = []

    def start(copy):
        copy.start()
        sends.append(copy)

    def slab_copy(way, q, d, hop):
        n = PIECES[q] if hop < 3 else PIECES[q] // 2
        lo = STARTS[q] + (way * n if hop == 3 else 0)
        ref = a_all.at[source(y, NY, way, d), pl.ds(lo, n)]
        return pltpu.make_async_remote_copy(
            src_ref=ref, dst_ref=ref, send_sem=as_sem.at[way, q, hop], recv_sem=ar_sem.at[way, q, hop],
            device_id=y_to[way], device_id_type=MESH)

    def inner_ref(p, way, d, core, half):
        n = BP // 2 if half else BP
        lo = core * BW + p * BP + (way * n if half else 0)
        return b_all.at[source(z, NZ, way, d), pl.ds(lo, n)]

    def inner_copy(p, way, d, hop):
        ref = inner_ref(p, way, d, c, hop == 3)
        return pltpu.make_async_remote_copy(
            src_ref=ref, dst_ref=ref, send_sem=bs_sem.at[p, way, hop], recv_sem=br_sem.at[p, way, hop],
            device_id=z_to[way], device_id_type=MESH)

    def core_copy(p, way, d, core):
        ref = inner_ref(p, way, d, core, d == 4)
        return pltpu.make_async_remote_copy(
            src_ref=ref, dst_ref=ref, send_sem=ss_sem.at[p, way, d], recv_sem=sr_sem.at[p, way, d],
            device_id=sibling, device_id_type=MESH)

    def part_copy(q, d):
        rows = pl.ds(STARTS[q], PIECES[q])
        return pltpu.make_async_remote_copy(
            src_ref=acc.at[(x + d) % NX, rows], dst_ref=rs.at[d - 1, rows],
            send_sem=cs_sem.at[q, d - 1], recv_sem=cr_sem.at[q, d - 1],
            device_id=x_to[d - 1], device_id_type=MESH)

    def send_slab(q):
        mask_slab(q)
        for way in range(2):
            start(slab_copy(way, q, 0, 0))

    def send_inner():
        mask_inner()
        for way, kind in enumerate((UP, DOWN)):
            meet(kind)
            for p in range(PB):
                start(inner_copy(p, way, 0, 0))

    def share_inner():
        meet(CORE)
        for p in range(PB):
            start(core_copy(p, 0, 0, c))

    def pass_slab(q, d):
        for way in range(2):
            slab_copy(way, q, d, d - 1).wait_recv()
            if d < 4:
                start(slab_copy(way, q, d, d))

    def pass_inner(p, d):
        for way in range(2):
            inner_copy(p, way, d, d - 1).wait_recv()
            if d < 4:
                start(inner_copy(p, way, d, d))
            start(core_copy(p, way, d, c))

    def wait_core():
        for d in range(5):
            for way in range(2 if d else 1):
                for p in range(PB):
                    core_copy(p, way, d, 1 - c).wait_recv()

    def multiply(q0, nq, d):
        rows = pl.ds(STARTS[q0], sum(PIECES[q0:q0 + nq]))
        for way in range(2 if 0 < d < 4 else 1):
            src = source(y, NY, way, d)
            product = jnp.dot(a_all[src, rows, :], b_all[src], preferred_element_type=jnp.float32)
            for k in range(NX):
                part = product[:, k * 128:(k + 1) * 128]
                acc[k, rows] = part if d == 0 else acc[k, rows] + part

    def send_parts(q):
        for d in (2, 1, 3):
            start(part_copy(q, d))

    def finish(q):
        for d in range(1, NX):
            part_copy(q, d).wait_recv()
        for i, lo, n in spans(q):
            rows = pl.ds(lo, n)
            total = acc[x, rows] + rs[0, rows] + rs[1, rows] + rs[2, rows]
            keep = col_ids[x // 2] >= row_ids[i]
            out[rows, :] = jnp.where(keep, total, 0.0).astype(jnp.bfloat16)

    def end():
        for copy in sends:
            copy.wait_send()

    def first_slab(q):
        mask_slab(q)
        enter()
        for way in range(2):
            start(slab_copy(way, q, 0, 0))
        reply()

    steps = {
        FIRST_SLAB: first_slab, SEND_SLAB: send_slab, SEND_INNER: send_inner, SHARE_INNER: share_inner,
        SLAB: pass_slab, INNER: pass_inner, WAIT_CORE: wait_core, MULTIPLY: multiply, MEET: meet,
        PARTS: send_parts, FINISH: finish, END: end,
    }

    def run(schedule):
        sends.clear()
        for name, *args in schedule:
            steps[name](*args)

    pl.when(z == 0)(lambda: run(FIRST_PLANE))
    pl.when(jnp.logical_and(z > 0, z <= 2))(lambda: run(NEAR_PLANES))
    pl.when(z > 2)(lambda: run(OTHER_PLANES))


def on_device(slab_panel, slab_pattern, inner_panel, inner_pattern, slab_rows, column_ids):
    whole = pl.BlockSpec(memory_space=pl.ANY)
    scalars = pl.BlockSpec(memory_space=pltpu.SMEM)
    dma = pltpu.SemaphoreType.DMA
    return pl.pallas_call(
        kernel,
        out_shape=jax.ShapeDtypeStruct((SIDE, 128), jnp.bfloat16),
        in_specs=[whole, scalars, whole, scalars, scalars, scalars],
        out_specs=pl.BlockSpec(memory_space=pltpu.VMEM),
        scratch_shapes=[
            pltpu.VMEM((SIDE, SIDE), jnp.bfloat16),
            pltpu.VMEM((BW, SIDE), jnp.bfloat16),
            pltpu.VMEM((NY, SIDE, SIDE), jnp.bfloat16),
            pltpu.VMEM((NZ, SIDE, SIDE), jnp.bfloat16),
            pltpu.VMEM((NX, SIDE, 128), jnp.float32),
            pltpu.VMEM((NX - 1, SIDE, 128), jnp.float32),
            pltpu.SemaphoreType.REGULAR((4,)),
            dma((Q + 1,)),
            dma((2, Q, 4)), dma((2, Q, 4)),
            dma((PB, 2, 4)), dma((PB, 2, 4)),
            dma((PB, 2, 5)), dma((PB, 2, 5)),
            dma((Q, NX - 1)), dma((Q, NX - 1)),
        ],
        compiler_params=pltpu.CompilerParams(
            collective_id=0, has_side_effects=True, vmem_limit_bytes=54976 * 1024),
    )(slab_panel.reshape(SIDE, SIDE), slab_pattern, inner_panel.reshape(BW, SIDE), inner_pattern,
      slab_rows, column_ids)


def solution(mesh):
    return jax.shard_map(
        on_device,
        mesh=mesh,
        in_specs=(
            P("row", "layer", "col"),
            P("row", "layer", "col"),
            P("layer", "row", "col"),
            P("layer", "row", "col"),
            P("row"),
            P("col"),
        ),
        out_specs=P("row", ("col", "layer")),
        check_vma=False,
    )
```
